512 devices in a mesh: ctx: 32 (over z_lo, y), head: 16 (over x, z_hi, core).
Axes of the slice: x: 4, y: 4, z: 16 (z_hi: 2, z_lo: 8; z = z_hi * 8 + z_lo), core: 2. Of those that a mesh axis runs over, the one named last changes fastest.
Arguments:
- q_nope: bfloat16 [4, 16384], P(None, 'head'), may hold values from -6 to 6
- q_rope: bfloat16 [4, 8192], P(None, 'head'), may hold values from -6 to 6
- latent_cache: bfloat16 [4, 16384, 512], P(None, 'ctx'), may hold values from -6 to 6
- rope_keys: bfloat16 [4, 64, 16384], P(None, None, 'ctx'), may hold values from -240 to 240
- lengths: int32 [4], replicated, may hold values from 2 to 16384, as said below
- w_uk: bfloat16 [128, 128, 512], P('head'), may hold values from -0.5 to 0.5
- w_uv: bfloat16 [128, 512, 128], P('head'), may hold values from -0.25 to 0.25
- w_o: bfloat16 [16384, 7168], P('head', 'ctx'), may hold values from -0.046875 to 0.046875
Outputs:
- layer_out: bfloat16 [4, 7168], P(None, 'ctx')
The draws below stay inside these ranges and needn't reach their ends.
Inputs may be any that keep to these rules, and one draw needn't show every extreme that they name: `lengths`: every sequence has at least two valid positions, and some sequence fills the whole capacity 16384.
All inputs are finite; a program needn't handle non-finite values.
Results may differ from the reference program's by a relative error of at most 0.014.
Values may be sent and summed in bfloat16 or wider, within the bound.
A program may use at most 64 MiB of HBM per device.

```python
import jax
import jax.numpy as jnp
from jax import lax

D = 7168
HEADS = 128
NOPE = 128
ROPE = 64
LATENT = 512
VHEAD = 128
ROWS = 4
TOKENS = 16384


def draw_q_rope(key, part):
    key = jax.random.fold_in(key, 11)
    noise = jnp.clip(jax.random.normal(key, (ROWS, HEADS, ROPE), jnp.float32), -6.0, 6.0)
    return noise.reshape(ROWS, HEADS * ROPE).astype(jnp.bfloat16)


def draw_rope_keys(key, part):
    key = jax.random.fold_in(key, 12)
    values = jnp.clip(jax.random.normal(key, (ROWS, ROPE, TOKENS), jnp.float32), -6.0, 6.0)
    return values.astype(jnp.bfloat16)


def draw_lengths(key, part):
    key = jax.random.fold_in(key, 13)
    first, second, third, fourth = jax.random.split(key, 4)
    one = jax.random.randint(first, (ROWS,), 2, TOKENS + 1)
    two = jax.random.randint(second, (ROWS,), 2, TOKENS + 1)
    three = jax.random.randint(third, (ROWS,), 2, TOKENS + 1)
    longest = jax.random.randint(fourth, (), 0, ROWS)
    drawn = jnp.minimum(jnp.minimum(one, two), three)
    return jnp.where(jnp.arange(ROWS) == longest, TOKENS, drawn).astype(jnp.int32)


def shard_levels(own_key, extent, shards, smallest, largest):
    gain = 1.0
    for dim, shards_of in shards:
        draws = jax.random.uniform(jax.random.fold_in(jax.random.fold_in(own_key, 6), dim), (shards_of,), jnp.float32, smallest / len(shards), largest / len(shards))
        gain = gain * jnp.repeat(jnp.exp(draws), extent[dim] // shards_of).reshape((-1,) + (1,) * (len(extent) - 1 - dim))
    return gain


def centred(own_key, extent, spread, reach, pieces=(), kind=jnp.bfloat16):
    gain = shard_levels(own_key, extent, pieces, -0.22, 0.18) if pieces else 1.0
    values = jax.random.normal(own_key, extent, jnp.float32) * spread * gain
    return jnp.minimum(jnp.maximum(values, -reach), reach).astype(kind)


def setup_inputs(seed: int = 0) -> dict:
    key_list = jax.random.split(jax.random.key(seed), 9)
    q_nope = centred(key_list[0], (ROWS, HEADS * NOPE), 1.0, 6.0, ((1, 16),))
    q_rope = draw_q_rope(jax.random.fold_in(key_list[8], 71), 0)
    latent_cache = centred(key_list[2], (ROWS, TOKENS, LATENT), 1.0, 6.0, ((1, 32),))
    rope_keys = draw_rope_keys(jax.random.fold_in(key_list[8], 71), 0)
    lengths = draw_lengths(jax.random.fold_in(key_list[8], 71), 0)
    w_uk = centred(key_list[5], (HEADS, NOPE, LATENT), NOPE ** -0.5, 0.5, ((0, 16),))
    w_uv = centred(key_list[6], (HEADS, LATENT, VHEAD), LATENT ** -0.5, 0.25, ((0, 16),))
    w_o = centred(key_list[7], (HEADS * VHEAD, D), (HEADS * VHEAD) ** -0.5, 0.046875, ((0, 16), (1, 32)))
    return dict(q_nope=q_nope, q_rope=q_rope, latent_cache=latent_cache, rope_keys=rope_keys, lengths=lengths, w_uk=w_uk, w_uv=w_uv, w_o=w_o)


def reference(q_nope, q_rope, latent_cache, rope_keys, lengths, w_uk, w_uv, w_o):
    scale = (NOPE + ROPE) ** -0.5
    queries = q_nope.reshape(ROWS, HEADS, NOPE).astype(jnp.float32)
    q_abs = jnp.einsum("rhn,hnc->rhc", queries, w_uk.astype(jnp.float32)).astype(jnp.bfloat16)
    rotary = q_rope.reshape(ROWS, HEADS, ROPE)

    def one_row(items):
        absorbed, rot, latent, keys, length = items
        latent_f = latent.astype(jnp.float32)
        scores = jnp.einsum("hc,tc->ht", absorbed.astype(jnp.float32), latent_f)
        scores = (scores + jnp.einsum("hp,pt->ht", rot.astype(jnp.float32), keys.astype(jnp.float32))) * scale
        valid = (jnp.arange(TOKENS, dtype=jnp.int32) < length)[None, :]
        scores = jnp.where(valid, scores, jnp.float32(-1e30))
        peak = jnp.max(scores, axis=1, keepdims=True)
        weights = jnp.where(valid, jnp.exp(scores - peak), jnp.float32(0.0))
        total = jnp.sum(weights, axis=1, keepdims=True)
        rounded = weights.astype(jnp.bfloat16).astype(jnp.float32)
        summed = jnp.einsum("ht,tc->hc", rounded, latent_f)
        return (summed / total).astype(jnp.bfloat16)

    attended = lax.map(one_row, (q_abs, rotary, latent_cache, rope_keys, lengths))
    head_values = jnp.einsum("rhc,hcv->rhv", attended.astype(jnp.float32), w_uv.astype(jnp.float32))
    head_values = head_values.astype(jnp.bfloat16).reshape(ROWS, HEADS * VHEAD)
    return jnp.dot(head_values, w_o, preferred_element_type=jnp.float32).astype(jnp.bfloat16)
```

```python
import functools

import jax
import jax.numpy as jnp
from jax import lax
from jax.experimental import pallas as pl
from jax.experimental.pallas import tpu as pltpu
from jax.sharding import PartitionSpec as P

MESH = pl.DeviceIdType.MESH
F32, BF16 = jnp.float32, jnp.bfloat16
LOW = -1e30
NT = (((1,), (1,)), ((), ()))
NN = (((1,), (0,)), ((), ()))


def dot(a, b, dims=NN):
    return lax.dot_general(a, b, dims, preferred_element_type=F32)


def iota(shape, dim):
    return lax.broadcasted_iota(jnp.int32, shape, dim)


def kernel(
    ny, nz, nhead,
    qn_hbm, qr_hbm, lat_hbm, keys_hbm, len_hbm, wuk_hbm, wuv_hbm, wo_hbm,
    out_ref,
    qn, qr, lat, keys, lens, wuk, wuv, wo,
    ysum, ystat, zsum, zstat, terms,
    in_sem, ysend, yrecv, zsend, zrecv, hsend, hrecv,
):
    rows, span, latent = lat.shape
    heads, nope, _ = wuk.shape
    rope = keys.shape[1]
    vwidth = wuv.shape[2]
    pairs = rows * heads
    ctx, head = lax.axis_index("ctx"), lax.axis_index("head")

    loads = [
        pltpu.make_async_copy(src, dst, in_sem.at[n])
        for n, (src, dst) in enumerate(
            [(qn_hbm, qn), (wuk_hbm, wuk), (qr_hbm, qr), (len_hbm, lens)]
            + [(keys_hbm, keys)]
            + [(lat_hbm.at[r], lat.at[r]) for r in range(rows)]
            + [(wuv_hbm, wuv), (wo_hbm, wo)]
        )
    ]
    for load in loads:
        load.start()
    l_qn, l_wuk, l_qr, l_len, l_keys = loads[:5]
    l_lat, l_wuv, l_wo = loads[5 : 5 + rows], loads[5 + rows], loads[6 + rows]

    ypeers = [{"ctx": ctx // ny * ny + lax.rem(ctx + k, ny), "head": head} for k in range(1, ny)]
    zpeers = [{"ctx": lax.rem(ctx + k * ny, ny * nz), "head": head} for k in range(1, nz)]
    hpeers = [{"ctx": ctx, "head": lax.rem(head + k, nhead)} for k in range(1, nhead)]
    barrier = pltpu.get_barrier_semaphore()
    for peer in zpeers + hpeers + ypeers:
        pl.semaphore_signal(barrier, inc=1, device_id=peer, device_id_type=MESH)

    l_qn.wait()
    q = qn[...].astype(F32)
    own = iota((heads, heads * nope), 1) // nope == iota((heads, heads * nope), 0)
    q = jnp.concatenate([jnp.where(own, q[r : r + 1], 0.0) for r in range(rows)], axis=0)
    l_wuk.wait()
    q_abs = dot(q.astype(BF16), wuk[...].reshape(heads * nope, latent))
    l_qr.wait()
    q = qr[...].astype(F32)
    own = iota((heads, heads * rope), 1) // rope == iota((heads, heads * rope), 0)
    q = jnp.concatenate([jnp.where(own, q[r : r + 1], 0.0) for r in range(rows)], axis=0)
    rotary = sum(q[:, n * 2 * rope : (n + 1) * 2 * rope] for n in range(heads // 2))

    l_len.wait()
    l_keys.wait()
    position = iota((heads, span), 1) + ctx * span
    scale = (nope + rope) ** -0.5
    peaks, totals, sums = [], [], []
    for r in range(rows):
        l_lat[r].wait()
        mine = slice(r * heads, (r + 1) * heads)
        s = dot(q_abs[mine].astype(BF16), lat[r], NT)
        s += dot(rotary[mine].astype(BF16), jnp.concatenate([keys[r], keys[r]], axis=0))
        valid = position < lens[r]
        s = jnp.where(valid, s * scale, LOW)
        peak = jnp.max(s, axis=1, keepdims=True)
        w = jnp.where(valid, jnp.exp(s - peak), 0.0)
        peaks.append(peak)
        totals.append(jnp.sum(w, axis=1, keepdims=True))
        sums.append(dot(w.astype(BF16), lat[r]))
    peak, total, summed = (jnp.concatenate(x, axis=0) for x in (peaks, totals, sums))

    l_wuv.wait()
    which = lax.rem(iota((pairs, latent), 0), heads)
    values = sum(
        dot(jnp.where(which == h, summed, 0.0).astype(BF16), wuv[h]) for h in range(heads)
    )

    lanes = 128
    eye = lax.rem(iota((pairs, lanes), 1), pairs) == iota((pairs, lanes), 0)
    per = lanes // pairs

    def as_row(column):
        return jnp.sum(jnp.where(eye, column, 0.0), axis=0, keepdims=True)

    def put(sums_ref, stat_ref, values, peak, total):
        sums_ref[pl.ds(0, pairs), :] = values.astype(BF16)
        stat_ref[pl.ds(0, 1), pl.ds(0, lanes)] = peak
        stat_ref[pl.ds(0, 1), pl.ds(lanes, lanes)] = total

    def exchange(sums_ref, stat_ref, peers, send, recv):
        copies = []
        for k, peer in reversed(list(enumerate(peers))):
            for j, (src, dst) in enumerate(
                [
                    (stat_ref.at[pl.ds(0, 1)], stat_ref.at[pl.ds(k + 1, 1)]),
                    (sums_ref.at[pl.ds(0, pairs)], sums_ref.at[pl.ds((k + 1) * pairs, pairs)]),
                ]
            ):
                copies.append(
                    pltpu.make_async_remote_copy(
                        src_ref=src, dst_ref=dst, send_sem=send.at[2 * k + j],
                        recv_sem=recv.at[2 * k + j], device_id=peer, device_id_type=MESH,
                    )
                )
                copies[-1].start()
        return copies

    def combine(sums_ref, stat_ref, n, last):
        peaks = stat_ref[:, pl.ds(0, lanes)]
        totals = stat_ref[:, pl.ds(lanes, lanes)]
        peak = jnp.max(peaks, axis=0, keepdims=True)
        factor = jnp.exp(peaks - peak)
        total = jnp.sum(totals * factor, axis=0, keepdims=True)
        if last:
            factor = factor / total
        block = iota((n, lanes), 1) // pairs
        values = 0.0
        for g in range(n // per):
            pick = block + g * per == iota((n, lanes), 0)
            row = jnp.sum(jnp.where(pick, factor, 0.0), axis=0, keepdims=True)
            weights = jnp.where(eye, row, 0.0)
            high = weights.astype(BF16)
            low = (weights - high.astype(F32)).astype(BF16)
            part = sums_ref[pl.ds(g * lanes, lanes), :]
            values = values + dot(high, part) + dot(low, part)
        return values, peak, total

    pl.semaphore_wait(barrier, len(ypeers) + len(zpeers) + len(hpeers))
    put(ysum, ystat, values, as_row(peak), as_row(total))
    ycopies = exchange(ysum, ystat, ypeers, ysend, yrecv)
    for copy in ycopies:
        copy.wait_recv()
    values, peak, total = combine(ysum, ystat, ny, False)

    put(zsum, zstat, values, peak, total)
    zcopies = exchange(zsum, zstat, zpeers, zsend, zrecv)
    for copy in zcopies:
        copy.wait_recv()
    values, peak, total = combine(zsum, zstat, nz, True)

    l_wo.wait()
    wide = jnp.concatenate([values] * heads, axis=1)
    which = iota((pairs, heads * vwidth), 1) // vwidth == lax.rem(
        iota((pairs, heads * vwidth), 0), heads
    )
    wide = jnp.where(which, wide, 0.0).astype(BF16)
    term = dot(wide, wo[...], NT)
    term = jnp.concatenate(
        [jnp.sum(term[r * heads : (r + 1) * heads], axis=0, keepdims=True) for r in range(rows)],
        axis=0,
    )
    terms[pl.ds(0, rows), :] = term[:, :lanes]
    terms[pl.ds(rows, rows), :] = jnp.concatenate(
        [term[:, lanes:], jnp.zeros((rows, 2 * lanes - term.shape[1]), F32)], axis=1
    )
    hcopies = []
    for k, peer in reversed(list(enumerate(hpeers))):
        hcopies.append(
            pltpu.make_async_remote_copy(
                src_ref=terms.at[pl.ds(0, 2 * rows)],
                dst_ref=terms.at[pl.ds((k + 1) * 2 * rows, 2 * rows)],
                send_sem=hsend.at[k], recv_sem=hrecv.at[k], device_id=peer, device_id_type=MESH,
            )
        )
        hcopies[-1].start()
    for copy in hcopies:
        copy.wait_recv()
    whole = sum(terms[pl.ds(k * 2 * rows, 2 * rows), :] for k in range(nhead))
    whole = jnp.concatenate([whole[:rows], whole[rows:]], axis=1)
    out_ref[...] = whole[:, : out_ref.shape[1]].astype(out_ref.dtype)
    for copy in ycopies + zcopies + hcopies:
        copy.wait_send()


def on_device(ny, nz, nhead, q_nope, q_rope, latent_cache, rope_keys, lengths, w_uk, w_uv, w_o):
    rows, heads = q_nope.shape[0], w_uk.shape[0]
    pairs, vwidth, width = rows * heads, w_uv.shape[2], w_o.shape[1]
    w_o = w_o.T
    args = (q_nope, q_rope, latent_cache, rope_keys, lengths, w_uk, w_uv, w_o)
    scratch = [
        pltpu.SMEM(a.shape, a.dtype) if a is lengths else pltpu.VMEM(a.shape, a.dtype) for a in args
    ]
    scratch += [
        pltpu.VMEM((ny * pairs, vwidth), BF16),
        pltpu.VMEM((ny, 256), F32),
        pltpu.VMEM((nz * pairs, vwidth), BF16),
        pltpu.VMEM((nz, 256), F32),
        pltpu.VMEM((nhead * 2 * rows, 128), F32),
        pltpu.SemaphoreType.DMA((len(args) + rows - 1,)),
    ]
    for n in (2 * (ny - 1), 2 * (nz - 1), nhead - 1):
        scratch += [pltpu.SemaphoreType.DMA((n,))] * 2
    return pl.pallas_call(
        functools.partial(kernel, ny, nz, nhead),
        out_shape=jax.ShapeDtypeStruct((rows, width), BF16),
        in_specs=[pl.BlockSpec(memory_space=pl.ANY)] * len(args),
        out_specs=pl.BlockSpec(memory_space=pltpu.VMEM),
        scratch_shapes=scratch,
        compiler_params=pltpu.CompilerParams(
            collective_id=0, has_side_effects=True, vmem_limit_bytes=60 * 1024 * 1024
        ),
        name="decode",
    )(*args)


def solution(mesh):
    placed = (
        P(None, "head"),
        P(None, "head"),
        P(None, "ctx", None),
        P(None, None, "ctx"),
        P(),
        P("head", None, None),
        P("head", None, None),
        P("head", "ctx"),
    )
    nhead, nctx = mesh.shape["head"], mesh.shape["ctx"]
    ny = 4
    body = functools.partial(on_device, ny, nctx // ny, nhead)
    return jax.shard_map(
        body, mesh=mesh, in_specs=placed, out_specs=P(None, "ctx"), check_vma=False
    )
```

```python
import functools

import jax
import jax.numpy as jnp
from jax import lax
from jax.experimental import pallas as pl
from jax.experimental.pallas import tpu as pltpu
from jax.sharding import PartitionSpec as P

MESH = pl.DeviceIdType.MESH
F32, BF16 = jnp.float32, jnp.bfloat16
LOW = -1e30
NT = (((1,), (1,)), ((), ()))
NN = (((1,), (0,)), ((), ()))


def dot(a, b, dims=NN):
    return lax.dot_general(a, b, dims, preferred_element_type=F32)


def iota(shape, dim):
    return lax.broadcasted_iota(jnp.int32, shape, dim)


def kernel(
    ny, nz, nhead,
    qn_hbm, qr_hbm, lat_hbm, keys_hbm, len_hbm, wuk_hbm, wuv_hbm, wo_hbm,
    out_ref,
    qn, qr, lat, keys, lens, wuk, wuv, wo,
    by_head, mixed, ysum, ystat, zsum, zstat, terms,
    in_sem, ysend, yrecv, zsend, zrecv, hsend, hrecv,
):
    rows, span, latent = lat.shape
    heads, nope, _ = wuk.shape
    rope = keys.shape[1]
    vwidth = wuv.shape[2]
    pairs = rows * heads
    ctx, head = lax.axis_index("ctx"), lax.axis_index("head")

    loads = [
        pltpu.make_async_copy(src, dst, in_sem.at[n])
        for n, (src, dst) in enumerate(
            [(qn_hbm, qn)]
            + [(wuk_hbm.at[pl.ds(2 * h, 2)], wuk.at[pl.ds(2 * h, 2)]) for h in range(heads // 2)]
            + [(qr_hbm, qr), (len_hbm, lens), (keys_hbm, keys)]
            + [(lat_hbm.at[r], lat.at[r]) for r in range(rows)]
            + [(wuv_hbm, wuv), (wo_hbm, wo)]
        )
    ]
    for load in loads:
        load.start()
    l_qn, l_wuk = loads[0], loads[1 : 1 + heads // 2]
    l_qr, l_len, l_keys = loads[1 + heads // 2 : 4 + heads // 2]
    l_lat, l_wuv, l_wo = loads[-2 - rows : -2], loads[-2], loads[-1]

    ypeers = [{"ctx": ctx // ny * ny + lax.rem(ctx + k, ny), "head": head} for k in range(1, ny)]
    zpeers = [{"ctx": lax.rem(ctx + k * ny, ny * nz), "head": head} for k in range(1, nz)]
    hpeers = [{"ctx": ctx, "head": lax.rem(head + k, nhead)} for k in range(1, nhead)]
    barrier = pltpu.get_barrier_semaphore()
    for peer in zpeers + hpeers + ypeers:
        pl.semaphore_signal(barrier, inc=1, device_id=peer, device_id_type=MESH)

    l_qn.wait()
    q = qn[...].astype(F32)
    row_head = iota((heads, 1), 0)
    q_abs = 0.0
    for j in range(heads // 2):
        part = jnp.concatenate(
            [
                jnp.concatenate(
                    [
                        jnp.where(row_head == h, q[r : r + 1, h * nope : (h + 1) * nope], 0.0)
                        for h in (2 * j, 2 * j + 1)
                    ],
                    axis=1,
                )
                for r in range(rows)
            ],
            axis=0,
        ).astype(BF16)
        l_wuk[j].wait()
        q_abs += dot(part, wuk[pl.ds(2 * j, 2)].reshape(2 * nope, latent))
    l_qr.wait()
    q = qr[...].astype(F32)
    lane = iota((heads, 2 * rope), 1)
    own = (lane >= rope) == ((iota((heads, 2 * rope), 0) & 1) == 1)
    rotary = jnp.concatenate(
        [
            sum(
                jnp.where(
                    own & (row_head >> 1 == n), q[r : r + 1, n * 2 * rope : (n + 1) * 2 * rope], 0.0
                )
                for n in range(heads // 2)
            )
            for r in range(rows)
        ],
        axis=0,
    )

    l_len.wait()
    l_keys.wait()
    position = iota((heads, span), 1) + ctx * span
    scale = (nope + rope) ** -0.5
    valid = jnp.concatenate([position < lens[r] for r in range(rows)], axis=0)
    scores = []
    for r in range(rows):
        mine = slice(r * heads, (r + 1) * heads)
        both = jnp.concatenate([keys[r], keys[r]], axis=0)
        scores.append(dot(rotary[mine].astype(BF16), both))
    for r in range(rows):
        mine = slice(r * heads, (r + 1) * heads)
        l_lat[r].wait()
        scores[r] += dot(q_abs[mine].astype(BF16), lat[r], NT)
    scores = jnp.where(valid, jnp.concatenate(scores, axis=0) * scale, LOW)
    peak = jnp.max(scores, axis=1, keepdims=True)
    weights = jnp.where(valid, jnp.exp(scores - peak), 0.0)
    total = jnp.sum(weights, axis=1, keepdims=True)
    for r in range(rows):
        mine = slice(r * heads, (r + 1) * heads)
        part = dot(weights[mine].astype(BF16), lat[r])
        for n in range(latent // 128):
            by_head[n, pl.ds(r * heads, heads), :] = part[:, n * 128 : (n + 1) * 128]
    l_wuv.wait()
    values = []
    for h in range(heads):
        mine = [by_head[n, pl.ds(h, rows, stride=heads), :] for n in range(latent // 128)]
        values.append(dot(jnp.concatenate(mine, axis=1).astype(BF16), wuv[h]))
    for h in range(heads):
        mixed[pl.ds(h, rows, stride=heads), :] = values[h]
    values = mixed[...]
    lanes = 128
    eye = (iota((pairs, lanes), 1) & (pairs - 1)) == iota((pairs, lanes), 0)
    per = lanes // pairs

    def as_row(column):
        return jnp.sum(jnp.where(eye, column, 0.0), axis=0, keepdims=True)

    def put(sums_ref, stat_ref, values, peak, total):
        sums_ref[pl.ds(0, pairs), :] = values.astype(BF16)
        stat_ref[pl.ds(0, 1), pl.ds(0, lanes)] = peak
        stat_ref[pl.ds(0, 1), pl.ds(lanes, lanes)] = total

    def exchange(sums_ref, stat_ref, peers, send, recv):
        copies = []
        for k, peer in reversed(list(enumerate(peers))):
            for j, (src, dst) in enumerate(
                [
                    (stat_ref.at[pl.ds(0, 1)], stat_ref.at[pl.ds(k + 1, 1)]),
                    (sums_ref.at[pl.ds(0, pairs)], sums_ref.at[pl.ds((k + 1) * pairs, pairs)]),
                ]
            ):
                pltpu.make_async_remote_copy(
                    src_ref=src, dst_ref=dst, send_sem=send.at[j], recv_sem=recv.at[j],
                    device_id=peer, device_id_type=MESH,
                ).start()
        n = len(peers)
        return [
            pltpu.make_async_remote_copy(
                src_ref=ref, dst_ref=ref, send_sem=send.at[j], recv_sem=recv.at[j],
                device_id=peers[0], device_id_type=MESH,
            )
            for j, ref in enumerate([stat_ref.at[pl.ds(1, n)], sums_ref.at[pl.ds(pairs, n * pairs)]])
        ]

    def combine(sums_ref, stat_ref, n, last):
        peaks = stat_ref[:, pl.ds(0, lanes)]
        totals = stat_ref[:, pl.ds(lanes, lanes)]
        peak = jnp.max(peaks, axis=0, keepdims=True)
        factor = jnp.exp(peaks - peak)
        total = jnp.sum(totals * factor, axis=0, keepdims=True)
        if last:
            factor = factor / total
        block = iota((n, lanes), 1) >> (pairs.bit_length() - 1)
        values = 0.0
        for g in range(n // per):
            pick = block + g * per == iota((n, lanes), 0)
            row = jnp.sum(jnp.where(pick, factor, 0.0), axis=0, keepdims=True)
            weights = jnp.where(eye, row, 0.0)
            high = weights.astype(BF16)
            low = (weights - high.astype(F32)).astype(BF16)
            part = sums_ref[pl.ds(g * lanes, lanes), :]
            values = values + dot(high, part) + dot(low, part)
        return values, peak, total

    pl.semaphore_wait(barrier, len(ypeers) + len(zpeers) + len(hpeers))
    put(ysum, ystat, values, as_row(peak), as_row(total))
    ycopies = exchange(ysum, ystat, ypeers, ysend, yrecv)
    for copy in ycopies:
        copy.wait_recv()
    values, peak, total = combine(ysum, ystat, ny, False)

    put(zsum, zstat, values, peak, total)
    zcopies = exchange(zsum, zstat, zpeers, zsend, zrecv)
    for copy in zcopies:
        copy.wait_recv()
    values, peak, total = combine(zsum, zstat, nz, True)

    l_wo.wait()
    mixed[...] = values
    wide = [mixed[pl.ds(h, rows, stride=heads), :] for h in range(heads)]
    term = dot(jnp.concatenate(wide, axis=1).astype(BF16), wo[...], NT)
    terms[pl.ds(0, rows), :] = term[:, :lanes]
    terms[pl.ds(rows, rows), :] = jnp.concatenate(
        [term[:, lanes:], jnp.zeros((rows, 2 * lanes - term.shape[1]), F32)], axis=1
    )
    for k, peer in reversed(list(enumerate(hpeers))):
        pltpu.make_async_remote_copy(
            src_ref=terms.at[pl.ds(0, 2 * rows)],
            dst_ref=terms.at[pl.ds((k + 1) * 2 * rows, 2 * rows)],
            send_sem=hsend.at[0], recv_sem=hrecv.at[0], device_id=peer, device_id_type=MESH,
        ).start()
    others = terms.at[pl.ds(2 * rows, (nhead - 1) * 2 * rows)]
    hcopy = pltpu.make_async_remote_copy(
        src_ref=others, dst_ref=others, send_sem=hsend.at[0], recv_sem=hrecv.at[0],
        device_id=hpeers[0], device_id_type=MESH,
    )
    hcopy.wait_recv()
    whole = sum(terms[pl.ds(k * 2 * rows, 2 * rows), :] for k in range(nhead))
    whole = jnp.concatenate([whole[:rows], whole[rows:]], axis=1)
    out_ref[...] = whole[:, : out_ref.shape[1]].astype(out_ref.dtype)
    for copy in ycopies + zcopies + [hcopy]:
        copy.wait_send()


def on_device(ny, nz, nhead, q_nope, q_rope, latent_cache, rope_keys, lengths, w_uk, w_uv, w_o):
    rows, heads = q_nope.shape[0], w_uk.shape[0]
    pairs, vwidth, width = rows * heads, w_uv.shape[2], w_o.shape[1]
    w_o = w_o.T
    args = (q_nope, q_rope, latent_cache, rope_keys, lengths, w_uk, w_uv, w_o)
    scratch = [
        pltpu.SMEM(a.shape, a.dtype) if a is lengths else pltpu.VMEM(a.shape, a.dtype) for a in args
    ]
    scratch += [
        pltpu.VMEM((w_uv.shape[1] // 128, pairs, 128), F32),
        pltpu.VMEM((pairs, vwidth), F32),
        pltpu.VMEM((ny * pairs, vwidth), BF16),
        pltpu.VMEM((ny, 256), F32),
        pltpu.VMEM((nz * pairs, vwidth), BF16),
        pltpu.VMEM((nz, 256), F32),
        pltpu.VMEM((nhead * 2 * rows, 128), F32),
        pltpu.SemaphoreType.DMA((len(args) + rows + heads // 2 - 2,)),
    ]
    for n in (2, 2, 1):
        scratch += [pltpu.SemaphoreType.DMA((n,))] * 2
    return pl.pallas_call(
        functools.partial(kernel, ny, nz, nhead),
        out_shape=jax.ShapeDtypeStruct((rows, width), BF16),
        in_specs=[pl.BlockSpec(memory_space=pl.ANY)] * len(args),
        out_specs=pl.BlockSpec(memory_space=pltpu.VMEM),
        scratch_shapes=scratch,
        compiler_params=pltpu.CompilerParams(
            collective_id=0, has_side_effects=True, vmem_limit_bytes=32 * 1024 * 1024
        ),
        name="decode",
    )(*(pltpu.with_memory_space_constraint(a, pltpu.HBM) for a in args))


def solution(mesh):
    placed = (
        P(None, "head"),
        P(None, "head"),
        P(None, "ctx", None),
        P(None, None, "ctx"),
        P(),
        P("head", None, None),
        P("head", None, None),
        P("head", "ctx"),
    )
    nhead, nctx = mesh.shape["head"], mesh.shape["ctx"]
    ny = 4
    body = functools.partial(on_device, ny, nctx // ny, nhead)
    return jax.shard_map(
        body, mesh=mesh, in_specs=placed, out_specs=P(None, "ctx"), check_vma=False
    )
```

```python
import functools

import jax
import jax.numpy as jnp
from jax import lax
from jax.experimental import pallas as pl
from jax.experimental.pallas import tpu as pltpu
from jax.sharding import PartitionSpec as P

MESH = pl.DeviceIdType.MESH
F32, BF16 = jnp.float32, jnp.bfloat16
LOW = -1e30
NT = (((1,), (1,)), ((), ()))
NN = (((1,), (0,)), ((), ()))


def dot(a, b, dims=NN):
    return lax.dot_general(a, b, dims, preferred_element_type=F32)


def iota(shape, dim):
    return lax.broadcasted_iota(jnp.int32, shape, dim)


def kernel(
    ny, nz, nhead,
    qn_hbm, qr_hbm, lat_hbm, keys_hbm, len_hbm, wuk_hbm, wuv_hbm, wo_hbm,
    out_ref,
    qn, qr, lat, keys, lens, wuk, wuv, wo,
    by_head, mixed, ysum, ystat, zsum, zstat, terms,
    run_sem, border_sem, in_sem, ysend, yrecv, zsend, zrecv, hsend, hrecv,
):
    rows, span, latent = lat.shape
    heads, nope, _ = wuk.shape
    rope = keys.shape[1]
    vwidth = wuv.shape[2]
    pairs = rows * heads
    ctx, head = lax.axis_index("ctx"), lax.axis_index("head")

    y, z = lax.rem(ctx, ny), lax.div(ctx, ny)
    half, core = lax.rem(lax.div(head, 2), 2), lax.rem(head, 2)
    column = lax.div(head, 4)

    def along(z):
        return {"ctx": z * ny + y, "head": head}

    def across(ctx, half, k, j):
        x = lax.rem(column + k, nhead // 4)
        return {"ctx": ctx, "head": x * 4 + half * 2 + lax.rem(core + j, 2)}

    ypeers = [{"ctx": z * ny + lax.rem(y + k, ny), "head": head} for k in range(1, ny)]
    zpeers = [along(lax.rem(z + k, nz)) for k in range(1, nz)]
    order = [(k, j) for k in (2, 1, 3, 0) for j in (1, 0)]
    hpeers = [across(ctx, 1 - half, k, j) for k, j in order]
    hpeers += [across(ctx, half, k, j) for k, j in order if k + j]
    beside = hpeers[len(order) :]
    middle = (nz // 2 - 1, nz // 2)
    at_middle = (z == middle[0]) | (z == middle[1])
    at_border = z == (nz - 1) * (1 - half)
    opposite = [across((nz - 1) * half * ny + y, 1 - half, k, j) for k, j in order]

    def tell(semaphore, peers):
        for peer in peers:
            pl.semaphore_signal(semaphore, inc=1, device_id=peer, device_id_type=MESH)

    barrier = pltpu.get_barrier_semaphore()
    for place in middle:
        pl.when(z != place)(functools.partial(tell, barrier, [along(place)]))
    pl.when(at_border)(functools.partial(tell, barrier, opposite))
    tell(barrier, ypeers + beside)

    loads = [
        pltpu.make_async_copy(src, dst, in_sem.at[n])
        for n, (src, dst) in enumerate(
            [(qn_hbm, qn)]
            + [(wuk_hbm.at[pl.ds(2 * h, 2)], wuk.at[pl.ds(2 * h, 2)]) for h in range(heads // 2)]
            + [(qr_hbm, qr), (len_hbm, lens), (keys_hbm, keys)]
            + [(lat_hbm.at[r], lat.at[r]) for r in range(rows)]
            + [(wuv_hbm, wuv), (wo_hbm, wo)]
        )
    ]
    for load in loads:
        load.start()
    l_qn, l_wuk = loads[0], loads[1 : 1 + heads // 2]
    l_qr, l_len, l_keys = loads[1 + heads // 2 : 4 + heads // 2]
    l_lat, l_wuv, l_wo = loads[-2 - rows : -2], loads[-2], loads[-1]

    l_qn.wait()
    q = qn[...].astype(F32)
    row_head = iota((heads, 1), 0)
    q_abs = 0.0
    for j in range(heads // 2):
        part = jnp.concatenate(
            [
                jnp.concatenate(
                    [
                        jnp.where(row_head == h, q[r : r + 1, h * nope : (h + 1) * nope], 0.0)
                        for h in (2 * j, 2 * j + 1)
                    ],
                    axis=1,
                )
                for r in range(rows)
            ],
            axis=0,
        ).astype(BF16)
        l_wuk[j].wait()
        q_abs += dot(part, wuk[pl.ds(2 * j, 2)].reshape(2 * nope, latent))
    l_qr.wait()
    q = qr[...].astype(F32)
    lane = iota((heads, 2 * rope), 1)
    own = (lane >= rope) == ((iota((heads, 2 * rope), 0) & 1) == 1)
    rotary = jnp.concatenate(
        [
            sum(
                jnp.where(
                    own & (row_head >> 1 == n), q[r : r + 1, n * 2 * rope : (n + 1) * 2 * rope], 0.0
                )
                for n in range(heads // 2)
            )
            for r in range(rows)
        ],
        axis=0,
    )

    l_len.wait()
    l_keys.wait()
    position = iota((heads, span), 1) + ctx * span
    scale = (nope + rope) ** -0.5
    valid = jnp.concatenate([position < lens[r] for r in range(rows)], axis=0)
    scores = []
    for r in range(rows):
        mine = slice(r * heads, (r + 1) * heads)
        both = jnp.concatenate([keys[r], keys[r]], axis=0)
        scores.append(dot(rotary[mine].astype(BF16), both))
    for r in range(rows):
        mine = slice(r * heads, (r + 1) * heads)
        l_lat[r].wait()
        scores[r] += dot(q_abs[mine].astype(BF16), lat[r], NT)
    scores = jnp.where(valid, jnp.concatenate(scores, axis=0) * scale, LOW)
    peak = jnp.max(scores, axis=1, keepdims=True)
    weights = jnp.where(valid, jnp.exp(scores - peak), 0.0)
    total = jnp.sum(weights, axis=1, keepdims=True)
    for r in range(rows):
        mine = slice(r * heads, (r + 1) * heads)
        part = dot(weights[mine].astype(BF16), lat[r])
        for n in range(latent // 128):
            by_head[n, pl.ds(r * heads, heads), :] = part[:, n * 128 : (n + 1) * 128]
    l_wuv.wait()
    values = []
    for h in range(heads):
        mine = [by_head[n, pl.ds(h, rows, stride=heads), :] for n in range(latent // 128)]
        values.append(dot(jnp.concatenate(mine, axis=1).astype(BF16), wuv[h]))
    for h in range(heads):
        mixed[pl.ds(h, rows, stride=heads), :] = values[h]
    values = mixed[...]
    lanes = 128
    eye = (iota((pairs, lanes), 1) & (pairs - 1)) == iota((pairs, lanes), 0)
    per = lanes // pairs

    def as_row(column):
        return jnp.sum(jnp.where(eye, column, 0.0), axis=0, keepdims=True)

    def put(sums_ref, stat_ref, values, peak, total):
        sums_ref[pl.ds(0, pairs), :] = values.astype(BF16)
        stat_ref[pl.ds(0, 1), pl.ds(0, lanes)] = peak
        stat_ref[pl.ds(0, 1), pl.ds(lanes, lanes)] = total

    def exchange(sums_ref, stat_ref, peers, send, recv):
        copies = []
        for k, peer in enumerate(peers):
            for j, (src, dst) in enumerate(
                [
                    (stat_ref.at[pl.ds(0, 1)], stat_ref.at[pl.ds(k + 1, 1)]),
                    (sums_ref.at[pl.ds(0, pairs)], sums_ref.at[pl.ds((k + 1) * pairs, pairs)]),
                ]
            ):
                pltpu.make_async_remote_copy(
                    src_ref=src, dst_ref=dst, send_sem=send.at[j], recv_sem=recv.at[j],
                    device_id=peer, device_id_type=MESH,
                ).start()
        n = len(peers)
        return [
            pltpu.make_async_remote_copy(
                src_ref=ref, dst_ref=ref, send_sem=send.at[j], recv_sem=recv.at[j],
                device_id=peers[0], device_id_type=MESH,
            )
            for j, ref in enumerate([stat_ref.at[pl.ds(1, n)], sums_ref.at[pl.ds(pairs, n * pairs)]])
        ]

    def combine(sums_ref, stat_ref, n, last):
        peaks = stat_ref[:, pl.ds(0, lanes)]
        totals = stat_ref[:, pl.ds(lanes, lanes)]
        peak = jnp.max(peaks, axis=0, keepdims=True)
        factor = jnp.exp(peaks - peak)
        total = jnp.sum(totals * factor, axis=0, keepdims=True)
        if last:
            factor = factor / total
        block = iota((n, lanes), 1) >> (pairs.bit_length() - 1)
        values = 0.0
        for g in range(n // per):
            pick = block + g * per == iota((n, lanes), 0)
            row = jnp.sum(jnp.where(pick, factor, 0.0), axis=0, keepdims=True)
            weights = jnp.where(eye, row, 0.0)
            high = weights.astype(BF16)
            low = (weights - high.astype(F32)).astype(BF16)
            part = sums_ref[pl.ds(g * lanes, lanes), :]
            values = values + dot(high, part) + dot(low, part)
        return values, peak, total

    heard = len(ypeers) + len(beside)
    heard += at_middle.astype(jnp.int32) * len(zpeers) + at_border.astype(jnp.int32) * len(opposite)
    pl.semaphore_wait(barrier, heard)

    @pl.when(at_middle)
    def _():
        first = lax.div(z, nz // 2) * (nz // 2 + 1)
        tell(run_sem, [along(first + k) for k in range(nz // 2 - 1)])

    put(ysum, ystat, values, as_row(peak), as_row(total))
    ycopies = exchange(ysum, ystat, ypeers, ysend, yrecv)
    for copy in ycopies:
        copy.wait_recv()
    values, peak, total = combine(ysum, ystat, ny, False)

    put(zsum, zstat, values, peak, total)

    @pl.when(jnp.logical_not(at_middle))
    def _():
        pl.semaphore_wait(run_sem, 1)

    @pl.when(at_border)
    def _():
        tell(border_sem, opposite)
        pl.semaphore_wait(border_sem, len(opposite))

    zcopies = exchange(zsum, zstat, zpeers, zsend, zrecv)
    for copy in zcopies:
        copy.wait_recv()
    values, peak, total = combine(zsum, zstat, nz, True)

    l_wo.wait()
    mixed[...] = values
    wide = [mixed[pl.ds(h, rows, stride=heads), :] for h in range(heads)]
    term = dot(jnp.concatenate(wide, axis=1).astype(BF16), wo[...], NT)
    terms[pl.ds(0, rows), :] = term[:, :lanes]
    terms[pl.ds(rows, rows), :] = jnp.concatenate(
        [term[:, lanes:], jnp.zeros((rows, 2 * lanes - term.shape[1]), F32)], axis=1
    )
    for k, peer in enumerate(hpeers):
        pltpu.make_async_remote_copy(
            src_ref=terms.at[pl.ds(0, 2 * rows)],
            dst_ref=terms.at[pl.ds((k + 1) * 2 * rows, 2 * rows)],
            send_sem=hsend.at[0], recv_sem=hrecv.at[0], device_id=peer, device_id_type=MESH,
        ).start()
    others = terms.at[pl.ds(2 * rows, (nhead - 1) * 2 * rows)]
    hcopy = pltpu.make_async_remote_copy(
        src_ref=others, dst_ref=others, send_sem=hsend.at[0], recv_sem=hrecv.at[0],
        device_id=hpeers[0], device_id_type=MESH,
    )
    hcopy.wait_recv()
    whole = sum(terms[pl.ds(k * 2 * rows, 2 * rows), :] for k in range(nhead))
    whole = jnp.concatenate([whole[:rows], whole[rows:]], axis=1)
    out_ref[...] = whole[:, : out_ref.shape[1]].astype(out_ref.dtype)
    for copy in ycopies + zcopies + [hcopy]:
        copy.wait_send()


def on_device(ny, nz, nhead, q_nope, q_rope, latent_cache, rope_keys, lengths, w_uk, w_uv, w_o):
    rows, heads = q_nope.shape[0], w_uk.shape[0]
    pairs, vwidth, width = rows * heads, w_uv.shape[2], w_o.shape[1]
    w_o = w_o.T
    args = (q_nope, q_rope, latent_cache, rope_keys, lengths, w_uk, w_uv, w_o)
    scratch = [
        pltpu.SMEM(a.shape, a.dtype) if a is lengths else pltpu.VMEM(a.shape, a.dtype) for a in args
    ]
    scratch += [
        pltpu.VMEM((w_uv.shape[1] // 128, pairs, 128), F32),
        pltpu.VMEM((pairs, vwidth), F32),
        pltpu.VMEM((ny * pairs, vwidth), BF16),
        pltpu.VMEM((ny, 256), F32),
        pltpu.VMEM((nz * pairs, vwidth), BF16),
        pltpu.VMEM((nz, 256), F32),
        pltpu.VMEM((nhead * 2 * rows, 128), F32),
        pltpu.SemaphoreType.REGULAR,
        pltpu.SemaphoreType.REGULAR,
        pltpu.SemaphoreType.DMA((len(args) + rows + heads // 2 - 2,)),
    ]
    for n in (2, 2, 1):
        scratch += [pltpu.SemaphoreType.DMA((n,))] * 2
    return pl.pallas_call(
        functools.partial(kernel, ny, nz, nhead),
        out_shape=jax.ShapeDtypeStruct((rows, width), BF16),
        in_specs=[pl.BlockSpec(memory_space=pl.ANY)] * len(args),
        out_specs=pl.BlockSpec(memory_space=pltpu.VMEM),
        scratch_shapes=scratch,
        compiler_params=pltpu.CompilerParams(
            collective_id=0, has_side_effects=True, vmem_limit_bytes=32 * 1024 * 1024
        ),
        name="decode",
    )(*(pltpu.with_memory_space_constraint(a, pltpu.HBM) for a in args))


def solution(mesh):
    placed = (
        P(None, "head"),
        P(None, "head"),
        P(None, "ctx", None),
        P(None, None, "ctx"),
        P(),
        P("head", None, None),
        P("head", None, None),
        P("head", "ctx"),
    )
    nhead, nctx = mesh.shape["head"], mesh.shape["ctx"]
    ny = 4
    body = functools.partial(on_device, ny, nctx // ny, nhead)
    return jax.shard_map(
        body, mesh=mesh, in_specs=placed, out_specs=P(None, "ctx"), check_vma=False
    )
```

```python
import functools

import jax
import jax.numpy as jnp
from jax import lax
from jax.experimental import pallas as pl
from jax.experimental.pallas import tpu as pltpu
from jax.sharding import PartitionSpec as P

MESH = pl.DeviceIdType.MESH
F32, BF16 = jnp.float32, jnp.bfloat16
LOW = -1e30
NT = (((1,), (1,)), ((), ()))
NN = (((1,), (0,)), ((), ()))


def dot(a, b, dims=NN):
    return lax.dot_general(a, b, dims, preferred_element_type=F32)


def iota(shape, dim):
    return lax.broadcasted_iota(jnp.int32, shape, dim)


def kernel(
    ny, nz, nhead,
    qn_hbm, qr_hbm, lat_hbm, keys_hbm, len_hbm, wuk_hbm, wuv_hbm, wo_hbm,
    out_ref,
    qn, qr, lat, keys, lens, wuk, wuv, wo,
    by_head, mixed, turned, asum, astat, bsum, bstat, terms,
    parity_sem, other_sem, border_sem, run_sem, in_sem, asend, arecv, bsend, brecv, hsend, hrecv,
):
    rows, span, latent = lat.shape
    heads, nope, _ = wuk.shape
    rope = keys.shape[1]
    vwidth = wuv.shape[2]
    pairs = rows * heads
    ctx, head = lax.axis_index("ctx"), lax.axis_index("head")

    loads = [
        pltpu.make_async_copy(src, dst, in_sem.at[n])
        for n, (src, dst) in enumerate(
            [(qn_hbm, qn)]
            + [(wuk_hbm.at[pl.ds(2 * h, 2)], wuk.at[pl.ds(2 * h, 2)]) for h in range(heads // 2)]
            + [(qr_hbm, qr), (len_hbm, lens), (keys_hbm, keys)]
            + [(lat_hbm.at[r], lat.at[r]) for r in range(rows)]
            + [(wuv_hbm, wuv), (wo_hbm, wo)]
        )
    ]
    for load in loads:
        load.start()
    l_qn, l_wuk = loads[0], loads[1 : 1 + heads // 2]
    l_qr, l_len, l_keys = loads[1 + heads // 2 : 4 + heads // 2]
    l_lat, l_wuv, l_wo = loads[-2 - rows : -2], loads[-2], loads[-1]

    y, z = lax.rem(ctx, ny), lax.div(ctx, ny)
    half, core = lax.rem(lax.div(head, 2), 2), lax.rem(head, 2)
    column, parity = lax.div(head, 4), lax.rem(z, 2)
    partner = z + 1 - 2 * parity

    def grid(z, k=0):
        return {"ctx": z * ny + lax.rem(y + k, ny), "head": head}

    def heads_at(z, half, k, j):
        x = lax.rem(column + k, nhead // 4)
        return {"ctx": z * ny + y, "head": x * 4 + half * 2 + lax.rem(core + j, 2)}

    apeers = [grid(z_, k) for z_, k in [(partner, 2), (partner, 1), (partner, 3), (z, 2), (z, 1), (z, 3), (partner, 0)]]
    bpeers = [grid(lax.rem(z + k, nz)) for k in range(2, nz, 2)]
    order = [(k, j) for k in (2, 1, 3, 0) for j in (1, 0)]
    distant = [heads_at(z, 1 - half, k, j) for k, j in order]
    beside = [heads_at(z, half, k, j) for k, j in order if k + j]

    upper = (z >= nz // 2).astype(jnp.int32)
    middle = (z >= nz // 4) & (z < nz - nz // 4)
    centre = (z == nz // 2 - 1) | (z == nz // 2)
    end = (z == 0) | (z == nz - 1)
    border = z == (nz - 1) * (1 - half)
    opposite = [heads_at((nz - 1) * half, 1 - half, k, j) for k, j in order]
    run = [grid(lax.rem(z + k, nz)) for k in range(1, nz)]

    def tell(semaphore, peers):
        for peer in peers:
            pl.semaphore_signal(semaphore, inc=1, device_id=peer, device_id_type=MESH)

    barrier = pltpu.get_barrier_semaphore()
    for place in (nz // 4, nz // 2):
        pl.when(z != place + parity)(functools.partial(tell, barrier, [grid(place + parity)]))
    pl.when(end)(functools.partial(tell, barrier, [grid(nz // 2 - 1 + upper)]))
    pl.when(border)(functools.partial(tell, barrier, opposite))
    tell(barrier, apeers + beside)

    l_qn.wait()
    q = qn[...].astype(F32)
    row_head = iota((heads, 1), 0)
    q_abs = 0.0
    for j in range(heads // 2):
        part = jnp.concatenate(
            [
                jnp.concatenate(
                    [
                        jnp.where(row_head == h, q[r : r + 1, h * nope : (h + 1) * nope], 0.0)
                        for h in (2 * j, 2 * j + 1)
                    ],
                    axis=1,
                )
                for r in range(rows)
            ],
            axis=0,
        ).astype(BF16)
        l_wuk[j].wait()
        q_abs += dot(part, wuk[pl.ds(2 * j, 2)].reshape(2 * nope, latent))
    l_qr.wait()
    q = qr[...].astype(F32)
    lane = iota((heads, 2 * rope), 1)
    own = (lane >= rope) == ((iota((heads, 2 * rope), 0) & 1) == 1)
    rotary = jnp.concatenate(
        [
            sum(
                jnp.where(
                    own & (row_head >> 1 == n), q[r : r + 1, n * 2 * rope : (n + 1) * 2 * rope], 0.0
                )
                for n in range(heads // 2)
            )
            for r in range(rows)
        ],
        axis=0,
    )

    l_len.wait()
    l_keys.wait()
    position = iota((heads, span), 1) + ctx * span
    scale = (nope + rope) ** -0.5
    valid = jnp.concatenate([position < lens[r] for r in range(rows)], axis=0)
    scores = []
    for r in range(rows):
        mine = slice(r * heads, (r + 1) * heads)
        both = jnp.concatenate([keys[r], keys[r]], axis=0)
        scores.append(dot(rotary[mine].astype(BF16), both))
    for r in range(rows):
        mine = slice(r * heads, (r + 1) * heads)
        if r % 2 == 0:
            l_lat[r].wait()
            l_lat[r + 1].wait()
        scores[r] += dot(q_abs[mine].astype(BF16), lat[r], NT)
    scores = jnp.where(valid, jnp.concatenate(scores, axis=0) * scale, LOW)
    peak = jnp.max(scores, axis=1, keepdims=True)
    weights = jnp.where(valid, jnp.exp(scores - peak), 0.0)
    total = jnp.sum(weights, axis=1, keepdims=True)
    for r in range(rows):
        mine = slice(r * heads, (r + 1) * heads)
        part = dot(weights[mine].astype(BF16), lat[r])
        for n in range(latent // 128):
            by_head[n, pl.ds(r * heads, heads), :] = part[:, n * 128 : (n + 1) * 128]
    l_wuv.wait()
    values = []
    for h in range(heads):
        mine = [by_head[n, pl.ds(h, rows, stride=heads), :] for n in range(latent // 128)]
        values.append(dot(jnp.concatenate(mine, axis=1).astype(BF16), wuv[h]))
    for h in range(heads):
        mixed[pl.ds(h, rows, stride=heads), :] = values[h]
    values = mixed[...]
    lanes = 128
    eye = (iota((pairs, lanes), 1) & (pairs - 1)) == iota((pairs, lanes), 0)
    per = lanes // pairs

    def as_row(column):
        return jnp.sum(jnp.where(eye, column, 0.0), axis=0, keepdims=True)

    def put(sums_ref, stat_ref, values, peak, total):
        sums_ref[pl.ds(0, pairs), :] = values.astype(BF16)
        stat_ref[pl.ds(0, 1), pl.ds(0, lanes)] = peak
        stat_ref[pl.ds(0, 1), pl.ds(lanes, lanes)] = total

    def exchange(sums_ref, stat_ref, peers, send, recv):
        copies = []
        for k, peer in enumerate(peers):
            for j, (src, dst) in enumerate(
                [
                    (stat_ref.at[pl.ds(0, 1)], stat_ref.at[pl.ds(k + 1, 1)]),
                    (sums_ref.at[pl.ds(0, pairs)], sums_ref.at[pl.ds((k + 1) * pairs, pairs)]),
                ]
            ):
                pltpu.make_async_remote_copy(
                    src_ref=src, dst_ref=dst, send_sem=send.at[j], recv_sem=recv.at[j],
                    device_id=peer, device_id_type=MESH,
                ).start()
        n = len(peers)
        return [
            pltpu.make_async_remote_copy(
                src_ref=ref, dst_ref=ref, send_sem=send.at[j], recv_sem=recv.at[j],
                device_id=peers[0], device_id_type=MESH,
            )
            for j, ref in enumerate([stat_ref.at[pl.ds(1, n)], sums_ref.at[pl.ds(pairs, n * pairs)]])
        ]

    def combine(sums_ref, stat_ref, n, last):
        peaks = stat_ref[:, pl.ds(0, lanes)]
        totals = stat_ref[:, pl.ds(lanes, lanes)]
        peak = jnp.max(peaks, axis=0, keepdims=True)
        factor = jnp.exp(peaks - peak)
        total = jnp.sum(totals * factor, axis=0, keepdims=True)
        if last:
            factor = factor / total
        block = iota((n, lanes), 1) >> (pairs.bit_length() - 1)
        values = 0.0
        for g in range(n // per):
            pick = block + g * per == iota((n, lanes), 0)
            row = jnp.sum(jnp.where(pick, factor, 0.0), axis=0, keepdims=True)
            weights = jnp.where(eye, row, 0.0)
            high = weights.astype(BF16)
            low = (weights - high.astype(F32)).astype(BF16)
            part = sums_ref[pl.ds(g * lanes, lanes), :]
            values = values + dot(high, part) + dot(low, part)
        return values, peak, total

    heard = len(apeers) + len(beside) + middle.astype(jnp.int32) * len(bpeers)
    heard += centre.astype(jnp.int32) + border.astype(jnp.int32) * len(opposite)
    pl.semaphore_wait(barrier, heard)
    pl.when(middle)(functools.partial(tell, parity_sem, [grid(z - 2 + 4 * upper)]))
    pl.when(centre)(functools.partial(tell, other_sem, [grid((nz - 1) * upper)]))

    put(asum, astat, values, as_row(peak), as_row(total))
    acopies = exchange(asum, astat, apeers, asend, arecv)
    l_wo.wait()
    turned[...] = wo[...].T
    for copy in acopies:
        copy.wait_recv()
    values, peak, total = combine(asum, astat, 2 * ny, False)
    put(bsum, bstat, values, peak, total)
    pl.when(jnp.logical_not(middle))(lambda: pl.semaphore_wait(parity_sem, 1))
    bcopies = exchange(bsum, bstat, bpeers, bsend, brecv)
    pl.when(end)(lambda: pl.semaphore_wait(other_sem, 1))

    @pl.when(border)
    def _():
        tell(border_sem, opposite)
        pl.semaphore_wait(border_sem, len(opposite))
        tell(run_sem, run)

    for copy in bcopies:
        copy.wait_recv()
    values, peak, total = combine(bsum, bstat, nz // 2, True)
    mixed[...] = values
    wide = [mixed[pl.ds(h, rows, stride=heads), :] for h in range(heads)]
    term = dot(jnp.concatenate(wide, axis=1).astype(BF16), turned[...])
    terms[pl.ds(0, rows), :] = term[:, :lanes]
    terms[pl.ds(rows, rows), :] = jnp.concatenate(
        [term[:, lanes:], jnp.zeros((rows, 2 * lanes - term.shape[1]), F32)], axis=1
    )

    def send_terms(first, peers):
        for k, peer in enumerate(peers):
            pltpu.make_async_remote_copy(
                src_ref=terms.at[pl.ds(0, 2 * rows)],
                dst_ref=terms.at[pl.ds((first + k) * 2 * rows, 2 * rows)],
                send_sem=hsend.at[0], recv_sem=hrecv.at[0], device_id=peer, device_id_type=MESH,
            ).start()

    pl.when(half == 0)(functools.partial(send_terms, 1 + len(distant), beside))
    pl.when(jnp.logical_not(border))(lambda: pl.semaphore_wait(run_sem, 1))
    send_terms(1, distant)
    pl.when(half == 1)(functools.partial(send_terms, 1 + len(distant), beside))
    others = terms.at[pl.ds(2 * rows, (nhead - 1) * 2 * rows)]
    hcopy = pltpu.make_async_remote_copy(
        src_ref=others, dst_ref=others, send_sem=hsend.at[0], recv_sem=hrecv.at[0],
        device_id=beside[0], device_id_type=MESH,
    )
    hcopy.wait_recv()
    whole = sum(terms[pl.ds(k * 2 * rows, 2 * rows), :] for k in range(nhead))
    whole = jnp.concatenate([whole[:rows], whole[rows:]], axis=1)
    out_ref[...] = whole[:, : out_ref.shape[1]].astype(out_ref.dtype)
    for copy in acopies + bcopies + [hcopy]:
        copy.wait_send()


def on_device(ny, nz, nhead, q_nope, q_rope, latent_cache, rope_keys, lengths, w_uk, w_uv, w_o):
    rows, heads = q_nope.shape[0], w_uk.shape[0]
    pairs, vwidth, width = rows * heads, w_uv.shape[2], w_o.shape[1]
    w_o = w_o.T
    args = (q_nope, q_rope, latent_cache, rope_keys, lengths, w_uk, w_uv, w_o)
    scratch = [
        pltpu.SMEM(a.shape, a.dtype) if a is lengths else pltpu.VMEM(a.shape, a.dtype) for a in args
    ]
    scratch += [
        pltpu.VMEM((w_uv.shape[1] // 128, pairs, 128), F32),
        pltpu.VMEM((pairs, vwidth), F32),
        pltpu.VMEM(w_o.shape[::-1], BF16),
        pltpu.VMEM((2 * ny * pairs, vwidth), BF16),
        pltpu.VMEM((2 * ny, 256), F32),
        pltpu.VMEM((nz // 2 * pairs, vwidth), BF16),
        pltpu.VMEM((nz // 2, 256), F32),
        pltpu.VMEM((nhead * 2 * rows, 128), F32),
        *[pltpu.SemaphoreType.REGULAR] * 4,
        pltpu.SemaphoreType.DMA((len(args) + rows + heads // 2 - 2,)),
    ]
    for n in (2, 2, 1):
        scratch += [pltpu.SemaphoreType.DMA((n,))] * 2
    return pl.pallas_call(
        functools.partial(kernel, ny, nz, nhead),
        out_shape=jax.ShapeDtypeStruct((rows, width), BF16),
        in_specs=[pl.BlockSpec(memory_space=pl.ANY)] * len(args),
        out_specs=pl.BlockSpec(memory_space=pltpu.VMEM),
        scratch_shapes=scratch,
        compiler_params=pltpu.CompilerParams(
            collective_id=0, has_side_effects=True, vmem_limit_bytes=32 * 1024 * 1024
        ),
        name="decode",
    )(*(pltpu.with_memory_space_constraint(a, pltpu.HBM) for a in args))


def solution(mesh):
    placed = (
        P(None, "head"),
        P(None, "head"),
        P(None, "ctx", None),
        P(None, None, "ctx"),
        P(),
        P("head", None, None),
        P("head", None, None),
        P("head", "ctx"),
    )
    nhead, nctx = mesh.shape["head"], mesh.shape["ctx"]
    ny = 4
    body = functools.partial(on_device, ny, nctx // ny, nhead)
    return jax.shard_map(
        body, mesh=mesh, in_specs=placed, out_specs=P(None, "ctx"), check_vma=False
    )
```

```python
import functools

import jax
import jax.numpy as jnp
from jax import lax
from jax.experimental import pallas as pl
from jax.experimental.pallas import tpu as pltpu
from jax.sharding import PartitionSpec as P

MESH = pl.DeviceIdType.MESH
F32, BF16 = jnp.float32, jnp.bfloat16
LOW = -1e30
NT = (((1,), (1,)), ((), ()))
NN = (((1,), (0,)), ((), ()))


def dot(a, b, dims=NN):
    return lax.dot_general(a, b, dims, preferred_element_type=F32)


def iota(shape, dim):
    return lax.broadcasted_iota(jnp.int32, shape, dim)


def kernel(
    ny, nz, nhead,
    qn_hbm, qr_hbm, lat_hbm, keys_hbm, len_hbm, wuk_hbm, wuv_hbm, wo_hbm,
    out_ref,
    qn, qr, lat, keys, lens, wuk, wuv, wo,
    by_head, mixed, turned, asum, astat, bsum, bstat, terms,
    parity_sem, other_sem, border_sem, run_sem, in_sem, asend, arecv, bsend, brecv, hsend, hrecv,
):
    rows, span, latent = lat.shape
    heads, nope, _ = wuk.shape
    rope = keys.shape[1]
    vwidth = wuv.shape[2]
    pairs = rows * heads
    ctx, head = lax.axis_index("ctx"), lax.axis_index("head")

    loads = [
        pltpu.make_async_copy(src, dst, in_sem.at[n])
        for n, (src, dst) in enumerate(
            [(qr_hbm, qr), (len_hbm, lens), (keys_hbm, keys), (qn_hbm, qn)]
            + [(wuk_hbm.at[pl.ds(4 * h, 4)], wuk.at[pl.ds(4 * h, 4)]) for h in range(heads // 4)]
            + [(lat_hbm.at[pl.ds(r, 2)], lat.at[pl.ds(r, 2)]) for r in range(0, rows, 2)]
            + [(wuv_hbm, wuv), (wo_hbm, wo)]
        )
    ]
    for load in loads:
        load.start()
    l_qr, l_len, l_keys, l_qn = loads[:4]
    l_wuk = loads[4 : 4 + heads // 4]
    l_lat, l_wuv, l_wo = loads[-2 - rows // 2 : -2], loads[-2], loads[-1]

    y, z = lax.rem(ctx, ny), lax.div(ctx, ny)
    half, core = lax.rem(lax.div(head, 2), 2), lax.rem(head, 2)
    column, parity = lax.div(head, 4), lax.rem(z, 2)
    partner = z + 1 - 2 * parity

    def grid(z, k=0):
        return {"ctx": z * ny + lax.rem(y + k, ny), "head": head}

    def heads_at(z, half, k, j):
        x = lax.rem(column + k, nhead // 4)
        return {"ctx": z * ny + y, "head": x * 4 + half * 2 + lax.rem(core + j, 2)}

    apeers = [grid(z_, k) for z_, k in [(partner, 2), (partner, 1), (partner, 3), (z, 2), (z, 1), (z, 3), (partner, 0)]]
    bpeers = [grid(lax.rem(z + k, nz)) for k in range(2, nz, 2)]
    order = [(k, j) for k in (2, 1, 3, 0) for j in (1, 0)]
    distant = [heads_at(z, 1 - half, k, j) for k, j in order]
    beside = [heads_at(z, half, k, j) for k, j in order if k + j]

    upper = (z >= nz // 2).astype(jnp.int32)
    middle = (z >= nz // 4) & (z < nz - nz // 4)
    centre = (z == nz // 2 - 1) | (z == nz // 2)
    end = (z == 0) | (z == nz - 1)
    border = z == (nz - 1) * (1 - half)
    opposite = [heads_at((nz - 1) * half, 1 - half, k, j) for k, j in order]
    run = [grid(lax.rem(z + k, nz)) for k in range(1, nz)]

    def tell(semaphore, peers):
        for peer in peers:
            pl.semaphore_signal(semaphore, inc=1, device_id=peer, device_id_type=MESH)

    barrier = pltpu.get_barrier_semaphore()
    for place in (nz // 4, nz // 2):
        pl.when(z != place + parity)(functools.partial(tell, barrier, [grid(place + parity)]))
    pl.when(end)(functools.partial(tell, barrier, [grid(nz // 2 - 1 + upper)]))
    pl.when(border)(functools.partial(tell, barrier, opposite))
    tell(barrier, apeers + beside)

    row_head = iota((heads, 1), 0)
    l_qr.wait()
    q = qr[...].astype(F32)
    lane = iota((heads, 2 * rope), 1)
    own = (lane >= rope) == ((iota((heads, 2 * rope), 0) & 1) == 1)
    rotary = jnp.concatenate(
        [
            sum(
                jnp.where(
                    own & (row_head >> 1 == n), q[r : r + 1, n * 2 * rope : (n + 1) * 2 * rope], 0.0
                )
                for n in range(heads // 2)
            )
            for r in range(rows)
        ],
        axis=0,
    )

    l_len.wait()
    l_keys.wait()
    position = iota((heads, span), 1) + ctx * span
    scale = (nope + rope) ** -0.5
    valid = jnp.concatenate([position < lens[r] for r in range(rows)], axis=0)
    scores = []
    for r in range(rows):
        mine = slice(r * heads, (r + 1) * heads)
        both = jnp.concatenate([keys[r], keys[r]], axis=0)
        scores.append(dot(rotary[mine].astype(BF16), both))
    l_qn.wait()
    q = qn[...].astype(F32)
    parts = [
        jnp.concatenate(
            [
                jnp.concatenate(
                    [
                        jnp.where(row_head == h, q[r : r + 1, h * nope : (h + 1) * nope], 0.0)
                        for h in (2 * j, 2 * j + 1)
                    ],
                    axis=1,
                )
                for r in range(rows)
            ],
            axis=0,
        ).astype(BF16)
        for j in range(heads // 2)
    ]
    q_abs = 0.0
    for j, part in enumerate(parts):
        if j % 2 == 0:
            l_wuk[j // 2].wait()
        q_abs += dot(part, wuk[pl.ds(2 * j, 2)].reshape(2 * nope, latent))
    for r in range(rows):
        mine = slice(r * heads, (r + 1) * heads)
        if r % 2 == 0:
            l_lat[r // 2].wait()
        scores[r] += dot(q_abs[mine].astype(BF16), lat[r], NT)
    scores = jnp.where(valid, jnp.concatenate(scores, axis=0) * scale, LOW)
    peak = jnp.max(scores, axis=1, keepdims=True)
    weights = jnp.where(valid, jnp.exp(scores - peak), 0.0)
    total = jnp.sum(weights, axis=1, keepdims=True)
    for r in range(rows):
        mine = slice(r * heads, (r + 1) * heads)
        part = dot(weights[mine].astype(BF16), lat[r])
        for n in range(latent // 128):
            by_head[n, pl.ds(r * heads, heads), :] = part[:, n * 128 : (n + 1) * 128]
    l_wuv.wait()
    values = []
    for h in range(heads):
        mine = [by_head[n, pl.ds(h, rows, stride=heads), :] for n in range(latent // 128)]
        values.append(dot(jnp.concatenate(mine, axis=1).astype(BF16), wuv[h]))
    for h in range(heads):
        mixed[pl.ds(h, rows, stride=heads), :] = values[h]
    values = mixed[...]
    lanes = 128
    eye = (iota((pairs, lanes), 1) & (pairs - 1)) == iota((pairs, lanes), 0)
    per = lanes // pairs

    def as_row(column):
        return jnp.sum(jnp.where(eye, column, 0.0), axis=0, keepdims=True)

    def put(sums_ref, stat_ref, values, peak, total):
        sums_ref[pl.ds(0, pairs), :] = values.astype(BF16)
        stat_ref[pl.ds(0, 1), pl.ds(0, lanes)] = peak
        stat_ref[pl.ds(0, 1), pl.ds(lanes, lanes)] = total

    def exchange(sums_ref, stat_ref, peers, send, recv):
        copies = []
        for k, peer in enumerate(peers):
            for j, (src, dst) in enumerate(
                [
                    (stat_ref.at[pl.ds(0, 1)], stat_ref.at[pl.ds(k + 1, 1)]),
                    (sums_ref.at[pl.ds(0, pairs)], sums_ref.at[pl.ds((k + 1) * pairs, pairs)]),
                ]
            ):
                pltpu.make_async_remote_copy(
                    src_ref=src, dst_ref=dst, send_sem=send.at[j], recv_sem=recv.at[j],
                    device_id=peer, device_id_type=MESH,
                ).start()
        n = len(peers)
        return [
            pltpu.make_async_remote_copy(
                src_ref=ref, dst_ref=ref, send_sem=send.at[j], recv_sem=recv.at[j],
                device_id=peers[0], device_id_type=MESH,
            )
            for j, ref in enumerate([stat_ref.at[pl.ds(1, n)], sums_ref.at[pl.ds(pairs, n * pairs)]])
        ]

    def combine(sums_ref, stat_ref, n, last):
        peaks = stat_ref[:, pl.ds(0, lanes)]
        totals = stat_ref[:, pl.ds(lanes, lanes)]
        peak = jnp.max(peaks, axis=0, keepdims=True)
        factor = jnp.exp(peaks - peak)
        total = jnp.sum(totals * factor, axis=0, keepdims=True)
        if last:
            factor = factor / total
        block = iota((n, lanes), 1) >> (pairs.bit_length() - 1)
        weights = []
        for g in range(n // per):
            pick = block + g * per == iota((n, lanes), 0)
            row = jnp.sum(jnp.where(pick, factor, 0.0), axis=0, keepdims=True)
            weights.append(jnp.where(eye, row, 0.0))
        weights = jnp.concatenate(weights, axis=1)
        high = weights.astype(BF16)
        low = (weights - high.astype(F32)).astype(BF16)
        both = dot(jnp.concatenate([high, low], axis=0), sums_ref[...])
        values = both[:pairs] + both[pairs:]
        return values, peak, total

    heard = len(apeers) + len(beside) + middle.astype(jnp.int32) * len(bpeers)
    heard += centre.astype(jnp.int32) + border.astype(jnp.int32) * len(opposite)
    pl.semaphore_wait(barrier, heard)
    pl.when(middle)(functools.partial(tell, parity_sem, [grid(z - 2 + 4 * upper)]))
    pl.when(centre)(functools.partial(tell, other_sem, [grid((nz - 1) * upper)]))

    put(asum, astat, values, as_row(peak), as_row(total))
    acopies = exchange(asum, astat, apeers, asend, arecv)
    l_wo.wait()
    turned[...] = wo[...].T
    for copy in acopies:
        copy.wait_recv()
    values, peak, total = combine(asum, astat, 2 * ny, False)
    put(bsum, bstat, values, peak, total)
    pl.when(jnp.logical_not(middle))(lambda: pl.semaphore_wait(parity_sem, 1))
    bcopies = exchange(bsum, bstat, bpeers, bsend, brecv)
    pl.when(end)(lambda: pl.semaphore_wait(other_sem, 1))

    @pl.when(border)
    def _():
        tell(border_sem, opposite)
        pl.semaphore_wait(border_sem, len(opposite))
        tell(run_sem, run)

    for copy in bcopies:
        copy.wait_recv()
    values, peak, total = combine(bsum, bstat, nz // 2, True)
    mixed[...] = values
    wide = [mixed[pl.ds(h, rows, stride=heads), :] for h in range(heads)]
    term = dot(jnp.concatenate(wide, axis=1).astype(BF16), turned[...])
    terms[pl.ds(0, rows), :] = term[:, :lanes]
    terms[pl.ds(rows, rows), :] = jnp.concatenate(
        [term[:, lanes:], jnp.zeros((rows, 2 * lanes - term.shape[1]), F32)], axis=1
    )

    def send_terms(first, peers):
        for k, peer in enumerate(peers):
            pltpu.make_async_remote_copy(
                src_ref=terms.at[pl.ds(0, 2 * rows)],
                dst_ref=terms.at[pl.ds((first + k) * 2 * rows, 2 * rows)],
                send_sem=hsend.at[0], recv_sem=hrecv.at[0], device_id=peer, device_id_type=MESH,
            ).start()

    pl.when(half == 0)(functools.partial(send_terms, 1 + len(distant), beside))
    pl.when(jnp.logical_not(border))(lambda: pl.semaphore_wait(run_sem, 1))
    send_terms(1, distant)
    pl.when(half == 1)(functools.partial(send_terms, 1 + len(distant), beside))
    others = terms.at[pl.ds(2 * rows, (nhead - 1) * 2 * rows)]
    hcopy = pltpu.make_async_remote_copy(
        src_ref=others, dst_ref=others, send_sem=hsend.at[0], recv_sem=hrecv.at[0],
        device_id=beside[0], device_id_type=MESH,
    )
    hcopy.wait_recv()
    whole = sum(terms[pl.ds(k * 2 * rows, 2 * rows), :] for k in range(nhead))
    whole = jnp.concatenate([whole[:rows], whole[rows:]], axis=1)
    out_ref[...] = whole[:, : out_ref.shape[1]].astype(out_ref.dtype)
    for copy in acopies + bcopies + [hcopy]:
        copy.wait_send()


def on_device(ny, nz, nhead, q_nope, q_rope, latent_cache, rope_keys, lengths, w_uk, w_uv, w_o):
    rows, heads = q_nope.shape[0], w_uk.shape[0]
    pairs, vwidth, width = rows * heads, w_uv.shape[2], w_o.shape[1]
    w_o = w_o.T
    args = (q_nope, q_rope, latent_cache, rope_keys, lengths, w_uk, w_uv, w_o)
    scratch = [
        pltpu.SMEM(a.shape, a.dtype) if a is lengths else pltpu.VMEM(a.shape, a.dtype) for a in args
    ]
    scratch += [
        pltpu.VMEM((w_uv.shape[1] // 128, pairs, 128), F32),
        pltpu.VMEM((pairs, vwidth), F32),
        pltpu.VMEM(w_o.shape[::-1], BF16),
        pltpu.VMEM((2 * ny * pairs, vwidth), BF16),
        pltpu.VMEM((2 * ny, 256), F32),
        pltpu.VMEM((nz // 2 * pairs, vwidth), BF16),
        pltpu.VMEM((nz // 2, 256), F32),
        pltpu.VMEM((nhead * 2 * rows, 128), F32),
        *[pltpu.SemaphoreType.REGULAR] * 4,
        pltpu.SemaphoreType.DMA((len(args) + rows // 2 + heads // 4 - 2,)),
    ]
    for n in (2, 2, 1):
        scratch += [pltpu.SemaphoreType.DMA((n,))] * 2
    return pl.pallas_call(
        functools.partial(kernel, ny, nz, nhead),
        out_shape=jax.ShapeDtypeStruct((rows, width), BF16),
        in_specs=[pl.BlockSpec(memory_space=pl.ANY)] * len(args),
        out_specs=pl.BlockSpec(memory_space=pltpu.VMEM),
        scratch_shapes=scratch,
        compiler_params=pltpu.CompilerParams(
            collective_id=0, has_side_effects=True, vmem_limit_bytes=32 * 1024 * 1024
        ),
        name="decode",
    )(*(pltpu.with_memory_space_constraint(a, pltpu.HBM) for a in args))


def solution(mesh):
    placed = (
        P(None, "head"),
        P(None, "head"),
        P(None, "ctx", None),
        P(None, None, "ctx"),
        P(),
        P("head", None, None),
        P("head", None, None),
        P("head", "ctx"),
    )
    nhead, nctx = mesh.shape["head"], mesh.shape["ctx"]
    ny = 4
    body = functools.partial(on_device, ny, nctx // ny, nhead)
    return jax.shard_map(
        body, mesh=mesh, in_specs=placed, out_specs=P(None, "ctx"), check_vma=False
    )
```

```python
import functools

import jax
import jax.numpy as jnp
from jax import lax
from jax.experimental import pallas as pl
from jax.experimental.pallas import tpu as pltpu
from jax.sharding import PartitionSpec as P

MESH = pl.DeviceIdType.MESH
F32, BF16 = jnp.float32, jnp.bfloat16
LOW = -1e30
NT = (((1,), (1,)), ((), ()))
NN = (((1,), (0,)), ((), ()))


def dot(a, b, dims=NN):
    return lax.dot_general(a, b, dims, preferred_element_type=F32)


def iota(shape, dim):
    return lax.broadcasted_iota(jnp.int32, shape, dim)


def kernel(
    ny, nz, nhead,
    qn_hbm, qr_hbm, lat_hbm, keys_hbm, len_hbm, wuk_hbm, wuv_hbm, wo_hbm,
    out_ref,
    qn, qr, lat, keys, lens, wuk, wuv, wo,
    by_head, mixed, turned, asum, astat, bsum, bstat, terms,
    parity_sem, other_sem, border_sem, run_sem, in_sem, asend, arecv, bsend, brecv, hsend, hrecv,
):
    rows, span, latent = lat.shape
    heads, nope, _ = wuk.shape
    rope = keys.shape[1]
    vwidth = wuv.shape[2]
    pairs = rows * heads
    ctx, head = lax.axis_index("ctx"), lax.axis_index("head")

    loads = [
        pltpu.make_async_copy(src, dst, in_sem.at[n])
        for n, (src, dst) in enumerate(
            [(qr_hbm, qr), (len_hbm, lens), (keys_hbm, keys), (qn_hbm, qn)]
            + [(wuk_hbm.at[pl.ds(4 * h, 4)], wuk.at[pl.ds(4 * h, 4)]) for h in range(heads // 4)]
            + [(lat_hbm.at[pl.ds(r, 2)], lat.at[pl.ds(r, 2)]) for r in range(0, rows, 2)]
            + [(wuv_hbm, wuv), (wo_hbm, wo)]
        )
    ]
    for load in loads:
        load.start()
    l_qr, l_len, l_keys, l_qn = loads[:4]
    l_wuk = loads[4 : 4 + heads // 4]
    l_lat, l_wuv, l_wo = loads[-2 - rows // 2 : -2], loads[-2], loads[-1]

    y, z = lax.rem(ctx, ny), lax.div(ctx, ny)
    half, core = lax.rem(lax.div(head, 2), 2), lax.rem(head, 2)
    column, parity = lax.div(head, 4), lax.rem(z, 2)
    partner = z + 1 - 2 * parity

    def grid(z, k=0):
        return {"ctx": z * ny + lax.rem(y + k, ny), "head": head}

    def heads_at(z, half, k, j):
        x = lax.rem(column + k, nhead // 4)
        return {"ctx": z * ny + y, "head": x * 4 + half * 2 + lax.rem(core + j, 2)}

    apeers = [grid(z_, k) for z_, k in [(partner, 2), (partner, 1), (partner, 3), (z, 2), (z, 1), (z, 3), (partner, 0)]]
    bpeers = [grid(lax.rem(z + k, nz)) for k in range(2, nz, 2)]
    order = [(k, j) for k in (2, 1, 3, 0) for j in (1, 0)]
    distant = [heads_at(z, 1 - half, k, j) for k, j in order]
    beside = [heads_at(z, half, k, j) for k, j in order if k + j]

    upper = (z >= nz // 2).astype(jnp.int32)
    middle = (z >= nz // 4) & (z < nz - nz // 4)
    centre = (z == nz // 2 - 1) | (z == nz // 2)
    end = (z == 0) | (z == nz - 1)
    border = z == (nz - 1) * (1 - half)
    opposite = [heads_at((nz - 1) * half, 1 - half, k, j) for k, j in order]
    run = [grid(lax.rem(z + k, nz)) for k in range(1, nz)]

    def tell(semaphore, peers):
        for peer in peers:
            pl.semaphore_signal(semaphore, inc=1, device_id=peer, device_id_type=MESH)

    barrier = pltpu.get_barrier_semaphore()
    for place in (nz // 4, nz // 2):
        pl.when(z != place + parity)(functools.partial(tell, barrier, [grid(place + parity)]))
    pl.when(end)(functools.partial(tell, barrier, [grid(nz // 2 - 1 + upper)]))
    pl.when(border)(functools.partial(tell, barrier, opposite))
    tell(barrier, apeers + beside)

    row_head = iota((heads, 1), 0)
    l_qr.wait()
    q = qr[...].astype(F32)
    lane = iota((heads, 2 * rope), 1)
    own = (lane >= rope) == ((iota((heads, 2 * rope), 0) & 1) == 1)
    rotary = jnp.concatenate(
        [
            sum(
                jnp.where(
                    own & (row_head >> 1 == n), q[r : r + 1, n * 2 * rope : (n + 1) * 2 * rope], 0.0
                )
                for n in range(heads // 2)
            )
            for r in range(rows)
        ],
        axis=0,
    )

    l_len.wait()
    l_keys.wait()
    position = iota((heads, span), 1) + ctx * span
    scale = (nope + rope) ** -0.5
    valid = jnp.concatenate([position < lens[r] for r in range(rows)], axis=0)
    scores = []
    for r in range(rows):
        mine = slice(r * heads, (r + 1) * heads)
        both = jnp.concatenate([keys[r], keys[r]], axis=0)
        scores.append(dot(rotary[mine].astype(BF16), both))
    l_qn.wait()
    q = qn[...].astype(F32)
    parts = [
        jnp.concatenate(
            [
                jnp.concatenate(
                    [
                        jnp.where(row_head == h, q[r : r + 1, h * nope : (h + 1) * nope], 0.0)
                        for h in (2 * j, 2 * j + 1)
                    ],
                    axis=1,
                )
                for r in range(rows)
            ],
            axis=0,
        ).astype(BF16)
        for j in range(heads // 2)
    ]
    q_abs = 0.0
    for j, part in enumerate(parts):
        if j % 2 == 0:
            l_wuk[j // 2].wait()
        q_abs += dot(part, wuk[pl.ds(2 * j, 2)].reshape(2 * nope, latent))
    for r in range(rows):
        mine = slice(r * heads, (r + 1) * heads)
        if r % 2 == 0:
            l_lat[r // 2].wait()
        scores[r] += dot(q_abs[mine].astype(BF16), lat[r], NT)
    scores = jnp.where(valid, jnp.concatenate(scores, axis=0) * scale, LOW)
    peak = jnp.max(scores, axis=1, keepdims=True)
    weights = jnp.where(valid, jnp.exp(scores - peak), 0.0)
    total = jnp.sum(weights, axis=1, keepdims=True)
    for r in range(rows):
        mine = slice(r * heads, (r + 1) * heads)
        part = dot(weights[mine].astype(BF16), lat[r])
        for n in range(latent // 128):
            by_head[n, pl.ds(r * heads, heads), :] = part[:, n * 128 : (n + 1) * 128]
    l_wuv.wait()
    values = []
    for h in range(heads):
        mine = [by_head[n, pl.ds(h, rows, stride=heads), :] for n in range(latent // 128)]
        values.append(dot(jnp.concatenate(mine, axis=1).astype(BF16), wuv[h]))
    for h in range(heads):
        mixed[pl.ds(h, rows, stride=heads), :] = values[h]
    values = mixed[...]
    lanes = 128
    eye = (iota((pairs, lanes), 1) & (pairs - 1)) == iota((pairs, lanes), 0)
    per = lanes // pairs

    def as_row(column):
        return jnp.sum(jnp.where(eye, column, 0.0), axis=0, keepdims=True)

    def put(sums_ref, stat_ref, values, peak, total):
        sums_ref[pl.ds(0, pairs), :] = values.astype(BF16)
        stat_ref[pl.ds(0, 1), pl.ds(0, lanes)] = peak
        stat_ref[pl.ds(0, 1), pl.ds(lanes, lanes)] = total

    def exchange(sums_ref, stat_ref, peers, send, recv):
        copies = []
        for k, peer in enumerate(peers):
            for j, (src, dst) in enumerate(
                [
                    (stat_ref.at[pl.ds(0, 1)], stat_ref.at[pl.ds(k + 1, 1)]),
                    (sums_ref.at[pl.ds(0, pairs)], sums_ref.at[pl.ds((k + 1) * pairs, pairs)]),
                ]
            ):
                pltpu.make_async_remote_copy(
                    src_ref=src, dst_ref=dst, send_sem=send.at[j], recv_sem=recv.at[j],
                    device_id=peer, device_id_type=MESH,
                ).start()
        n = len(peers)
        return [
            pltpu.make_async_remote_copy(
                src_ref=ref, dst_ref=ref, send_sem=send.at[j], recv_sem=recv.at[j],
                device_id=peers[0], device_id_type=MESH,
            )
            for j, ref in enumerate([stat_ref.at[pl.ds(1, n)], sums_ref.at[pl.ds(pairs, n * pairs)]])
        ]

    def combine(sums_ref, stat_ref, n, last):
        peaks = stat_ref[:, pl.ds(0, lanes)]
        totals = stat_ref[:, pl.ds(lanes, lanes)]
        peak = jnp.max(peaks, axis=0, keepdims=True)
        factor = jnp.exp(peaks - peak)
        total = jnp.sum(totals * factor, axis=0, keepdims=True)
        if last:
            factor = factor / total
        block = iota((n, lanes), 1) >> (pairs.bit_length() - 1)
        weights = []
        for g in range(n // per):
            pick = block + g * per == iota((n, lanes), 0)
            row = jnp.sum(jnp.where(pick, factor, 0.0), axis=0, keepdims=True)
            weights.append(jnp.where(eye, row, 0.0))
        weights = jnp.concatenate(weights, axis=1)
        high = weights.astype(BF16)
        low = (weights - high.astype(F32)).astype(BF16)
        both = dot(jnp.concatenate([high, low], axis=0), sums_ref[...])
        values = both[:pairs] + both[pairs:]
        return values, peak, total

    heard = len(apeers) + len(beside) + middle.astype(jnp.int32) * len(bpeers)
    heard += centre.astype(jnp.int32) + border.astype(jnp.int32) * len(opposite)
    pl.semaphore_wait(barrier, heard)
    pl.when(middle)(functools.partial(tell, parity_sem, [grid(z - 2 + 4 * upper)]))
    pl.when(centre)(functools.partial(tell, other_sem, [grid((nz - 1) * upper)]))

    put(asum, astat, values, as_row(peak), as_row(total))
    acopies = exchange(asum, astat, apeers, asend, arecv)
    l_wo.wait()
    turned[...] = wo[...].T
    for copy in acopies:
        copy.wait_recv()
    values, peak, total = combine(asum, astat, 2 * ny, False)
    put(bsum, bstat, values, peak, total)
    pl.when(jnp.logical_not(middle))(lambda: pl.semaphore_wait(parity_sem, 1))
    bcopies = exchange(bsum, bstat, bpeers, bsend, brecv)
    pl.when(end)(lambda: pl.semaphore_wait(other_sem, 1))

    @pl.when(border)
    def _():
        tell(border_sem, opposite)
        pl.semaphore_wait(border_sem, len(opposite))
        tell(run_sem, run)

    for copy in bcopies:
        copy.wait_recv()
    values, peak, total = combine(bsum, bstat, nz // 2, True)
    mixed[...] = values
    wide = [mixed[pl.ds(h, rows, stride=heads), :] for h in range(heads)]
    term = dot(jnp.concatenate(wide, axis=1).astype(BF16), turned[...])
    terms[pl.ds(0, rows), :] = term[:, :lanes]
    terms[pl.ds(rows, rows), :] = jnp.concatenate(
        [term[:, lanes:], jnp.zeros((rows, 2 * lanes - term.shape[1]), F32)], axis=1
    )

    def send_terms(first, peers, kind):
        for k, peer in enumerate(peers):
            pltpu.make_async_remote_copy(
                src_ref=terms.at[pl.ds(0, 2 * rows)],
                dst_ref=terms.at[pl.ds((first + k) * 2 * rows, 2 * rows)],
                send_sem=hsend.at[kind], recv_sem=hrecv.at[kind], device_id=peer, device_id_type=MESH,
            ).start()

    def arrival(first, peers, kind):
        part = terms.at[pl.ds(first * 2 * rows, len(peers) * 2 * rows)]
        return pltpu.make_async_remote_copy(
            src_ref=part, dst_ref=part, send_sem=hsend.at[kind], recv_sem=hrecv.at[kind],
            device_id=peers[0], device_id_type=MESH,
        )

    hcopies = [arrival(1, distant, 0), arrival(1 + len(distant), beside, 1)]

    @pl.when(half == 0)
    def _():
        send_terms(1 + len(distant), beside, 1)
        hcopies[1].wait_recv()

    pl.when(jnp.logical_not(border))(lambda: pl.semaphore_wait(run_sem, 1))
    send_terms(1, distant, 0)

    @pl.when(half == 1)
    def _():
        send_terms(1 + len(distant), beside, 1)
        hcopies[1].wait_recv()

    hcopies[0].wait_recv()
    whole = sum(terms[pl.ds(k * 2 * rows, 2 * rows), :] for k in range(nhead))
    whole = jnp.concatenate([whole[:rows], whole[rows:]], axis=1)
    out_ref[...] = whole[:, : out_ref.shape[1]].astype(out_ref.dtype)
    for copy in acopies + bcopies + hcopies:
        copy.wait_send()


def on_device(ny, nz, nhead, q_nope, q_rope, latent_cache, rope_keys, lengths, w_uk, w_uv, w_o):
    rows, heads = q_nope.shape[0], w_uk.shape[0]
    pairs, vwidth, width = rows * heads, w_uv.shape[2], w_o.shape[1]
    w_o = w_o.T
    args = (q_nope, q_rope, latent_cache, rope_keys, lengths, w_uk, w_uv, w_o)
    scratch = [
        pltpu.SMEM(a.shape, a.dtype) if a is lengths else pltpu.VMEM(a.shape, a.dtype) for a in args
    ]
    scratch += [
        pltpu.VMEM((w_uv.shape[1] // 128, pairs, 128), F32),
        pltpu.VMEM((pairs, vwidth), F32),
        pltpu.VMEM(w_o.shape[::-1], BF16),
        pltpu.VMEM((2 * ny * pairs, vwidth), BF16),
        pltpu.VMEM((2 * ny, 256), F32),
        pltpu.VMEM((nz // 2 * pairs, vwidth), BF16),
        pltpu.VMEM((nz // 2, 256), F32),
        pltpu.VMEM((nhead * 2 * rows, 128), F32),
        *[pltpu.SemaphoreType.REGULAR] * 4,
        pltpu.SemaphoreType.DMA((len(args) + rows // 2 + heads // 4 - 2,)),
    ]
    for n in (2, 2, 2):
        scratch += [pltpu.SemaphoreType.DMA((n,))] * 2
    return pl.pallas_call(
        functools.partial(kernel, ny, nz, nhead),
        out_shape=jax.ShapeDtypeStruct((rows, width), BF16),
        in_specs=[pl.BlockSpec(memory_space=pl.ANY)] * len(args),
        out_specs=pl.BlockSpec(memory_space=pltpu.VMEM),
        scratch_shapes=scratch,
        compiler_params=pltpu.CompilerParams(
            collective_id=0, has_side_effects=True, vmem_limit_bytes=32 * 1024 * 1024
        ),
        name="decode",
    )(*(pltpu.with_memory_space_constraint(a, pltpu.HBM) for a in args))


def solution(mesh):
    placed = (
        P(None, "head"),
        P(None, "head"),
        P(None, "ctx", None),
        P(None, None, "ctx"),
        P(),
        P("head", None, None),
        P("head", None, None),
        P("head", "ctx"),
    )
    nhead, nctx = mesh.shape["head"], mesh.shape["ctx"]
    ny = 4
    body = functools.partial(on_device, ny, nctx // ny, nhead)
    return jax.shard_map(
        body, mesh=mesh, in_specs=placed, out_specs=P(None, "ctx"), check_vma=False
    )
```

```python
import functools

import jax
import jax.numpy as jnp
from jax import lax
from jax.experimental import pallas as pl
from jax.experimental.pallas import tpu as pltpu
from jax.sharding import PartitionSpec as P

MESH = pl.DeviceIdType.MESH
F32, BF16 = jnp.float32, jnp.bfloat16
LOW = -1e30
NT = (((1,), (1,)), ((), ()))
NN = (((1,), (0,)), ((), ()))


def dot(a, b, dims=NN):
    return lax.dot_general(a, b, dims, preferred_element_type=F32)


def iota(shape, dim):
    return lax.broadcasted_iota(jnp.int32, shape, dim)


def kernel(
    ny, nz, nhead,
    qn_hbm, qr_hbm, lat_hbm, keys_hbm, len_hbm, wuk_hbm, wuv_hbm, wo_hbm,
    out_ref,
    qn, qr, lat, keys, lens, wuk, wuv, wo,
    by_head, mixed, turned, asum, astat, bsum, bstat, terms,
    parity_sem, other_sem, border_sem, run_sem, in_sem, asend, arecv, bsend, brecv, hsend, hrecv,
):
    rows, span, latent = lat.shape
    heads, nope, _ = wuk.shape
    rope = keys.shape[1]
    vwidth = wuv.shape[2]
    pairs = rows * heads
    ctx, head = lax.axis_index("ctx"), lax.axis_index("head")

    loads = [
        pltpu.make_async_copy(src, dst, in_sem.at[n])
        for n, (src, dst) in enumerate(
            [(qr_hbm, qr), (len_hbm, lens), (keys_hbm, keys), (qn_hbm, qn)]
            + [(wuk_hbm.at[pl.ds(4 * h, 4)], wuk.at[pl.ds(4 * h, 4)]) for h in range(heads // 4)]
            + [(lat_hbm.at[pl.ds(r, 2)], lat.at[pl.ds(r, 2)]) for r in range(0, rows, 2)]
            + [(wuv_hbm, wuv), (wo_hbm, wo)]
        )
    ]
    for load in loads:
        load.start()
    l_qr, l_len, l_keys, l_qn = loads[:4]
    l_wuk = loads[4 : 4 + heads // 4]
    l_lat, l_wuv, l_wo = loads[-2 - rows // 2 : -2], loads[-2], loads[-1]

    y, z = lax.rem(ctx, ny), lax.div(ctx, ny)
    half, core = lax.rem(lax.div(head, 2), 2), lax.rem(head, 2)
    column, parity = lax.div(head, 4), lax.rem(z, 2)
    partner = z + 1 - 2 * parity

    def grid(z, k=0):
        return {"ctx": z * ny + lax.rem(y + k, ny), "head": head}

    def heads_at(z, half, k, j):
        x = lax.rem(column + k, nhead // 4)
        return {"ctx": z * ny + y, "head": x * 4 + half * 2 + lax.rem(core + j, 2)}

    apeers = [grid(z_, k) for z_, k in [(partner, 2), (partner, 1), (partner, 3), (z, 2), (z, 1), (z, 3), (partner, 0)]]
    bpeers = [grid(lax.rem(z + k, nz)) for k in range(2, nz, 2)]
    order = [(k, j) for k in (2, 1, 3, 0) for j in (1, 0)]
    distant = [heads_at(z, 1 - half, k, j) for k, j in order]
    beside = [heads_at(z, half, k, j) for k, j in order if k + j]

    upper = (z >= nz // 2).astype(jnp.int32)
    middle = (z >= nz // 4) & (z < nz - nz // 4)
    centre = (z == nz // 2 - 1) | (z == nz // 2)
    end = (z == 0) | (z == nz - 1)
    border = z == (nz - 1) * (1 - half)
    opposite = [heads_at((nz - 1) * half, 1 - half, k, j) for k, j in order]
    run = [grid(lax.rem(z + k, nz)) for k in range(1, nz)]

    def tell(semaphore, peers):
        for peer in peers:
            pl.semaphore_signal(semaphore, inc=1, device_id=peer, device_id_type=MESH)

    barrier = pltpu.get_barrier_semaphore()
    for place in (nz // 4, nz // 2):
        pl.when(z != place + parity)(functools.partial(tell, barrier, [grid(place + parity)]))
    pl.when(end)(functools.partial(tell, barrier, [grid(nz // 2 - 1 + upper)]))
    pl.when(border)(functools.partial(tell, barrier, opposite))
    tell(barrier, apeers + beside)

    row_head = iota((heads, 1), 0)
    l_qr.wait()
    q = qr[...].astype(F32)
    lane = iota((heads, 2 * rope), 1)
    own = (lane >= rope) == ((iota((heads, 2 * rope), 0) & 1) == 1)
    rotary = jnp.concatenate(
        [
            sum(
                jnp.where(
                    own & (row_head >> 1 == n), q[r : r + 1, n * 2 * rope : (n + 1) * 2 * rope], 0.0
                )
                for n in range(heads // 2)
            )
            for r in range(rows)
        ],
        axis=0,
    )

    l_len.wait()
    l_keys.wait()
    position = iota((heads, span), 1) + ctx * span
    scale = (nope + rope) ** -0.5
    valid = jnp.concatenate([position < lens[r] for r in range(rows)], axis=0)
    scores = []
    for r in range(rows):
        mine = slice(r * heads, (r + 1) * heads)
        both = jnp.concatenate([keys[r], keys[r]], axis=0)
        scores.append(dot(rotary[mine].astype(BF16), both))
    l_qn.wait()
    q = qn[...].astype(F32)
    parts = [
        jnp.concatenate(
            [
                jnp.concatenate(
                    [
                        jnp.where(row_head == h, q[r : r + 1, h * nope : (h + 1) * nope], 0.0)
                        for h in (2 * j, 2 * j + 1)
                    ],
                    axis=1,
                )
                for r in range(rows)
            ],
            axis=0,
        ).astype(BF16)
        for j in range(heads // 2)
    ]
    q_abs = 0.0
    for j, part in enumerate(parts):
        if j % 2 == 0:
            l_wuk[j // 2].wait()
        q_abs += dot(part, wuk[pl.ds(2 * j, 2)].reshape(2 * nope, latent))
    for r in range(rows):
        mine = slice(r * heads, (r + 1) * heads)
        if r % 2 == 0:
            l_lat[r // 2].wait()
        scores[r] += dot(q_abs[mine].astype(BF16), lat[r], NT)
    scores = jnp.where(valid, jnp.concatenate(scores, axis=0) * scale, LOW)
    peak = jnp.max(scores, axis=1, keepdims=True)
    weights = jnp.where(valid, jnp.exp(scores - peak), 0.0)
    total = jnp.sum(weights, axis=1, keepdims=True)
    for r in range(rows):
        mine = slice(r * heads, (r + 1) * heads)
        part = dot(weights[mine].astype(BF16), lat[r])
        for n in range(latent // 128):
            by_head[n, pl.ds(r * heads, heads), :] = part[:, n * 128 : (n + 1) * 128]
    l_wuv.wait()
    values = []
    for h in range(heads):
        mine = [by_head[n, pl.ds(h, rows, stride=heads), :] for n in range(latent // 128)]
        values.append(dot(jnp.concatenate(mine, axis=1).astype(BF16), wuv[h]))
    for h in range(heads):
        mixed[pl.ds(h, rows, stride=heads), :] = values[h]
    values = mixed[...]
    lanes = 128
    eye = (iota((pairs, lanes), 1) & (pairs - 1)) == iota((pairs, lanes), 0)
    per = lanes // pairs

    def as_row(column):
        return jnp.sum(jnp.where(eye, column, 0.0), axis=0, keepdims=True)

    def put(sums_ref, stat_ref, values, peak, total):
        sums_ref[pl.ds(0, pairs), :] = values.astype(BF16)
        stat_ref[pl.ds(0, 1), pl.ds(0, lanes)] = peak
        stat_ref[pl.ds(0, 1), pl.ds(lanes, lanes)] = total

    def exchange(sums_ref, stat_ref, peers, send, recv):
        copies = []
        for k, peer in enumerate(peers):
            for j, (src, dst) in enumerate(
                [
                    (stat_ref.at[pl.ds(0, 1)], stat_ref.at[pl.ds(k + 1, 1)]),
                    (sums_ref.at[pl.ds(0, pairs)], sums_ref.at[pl.ds((k + 1) * pairs, pairs)]),
                ]
            ):
                pltpu.make_async_remote_copy(
                    src_ref=src, dst_ref=dst, send_sem=send.at[j], recv_sem=recv.at[j],
                    device_id=peer, device_id_type=MESH,
                ).start()
        n = len(peers)
        return [
            pltpu.make_async_remote_copy(
                src_ref=ref, dst_ref=ref, send_sem=send.at[j], recv_sem=recv.at[j],
                device_id=peers[0], device_id_type=MESH,
            )
            for j, ref in enumerate([stat_ref.at[pl.ds(1, n)], sums_ref.at[pl.ds(pairs, n * pairs)]])
        ]

    def combine(sums_ref, stat_ref, n, last):
        peaks = stat_ref[:, pl.ds(0, lanes)]
        totals = stat_ref[:, pl.ds(lanes, lanes)]
        peak = jnp.max(peaks, axis=0, keepdims=True)
        factor = jnp.exp(peaks - peak)
        total = jnp.sum(totals * factor, axis=0, keepdims=True)
        if last:
            factor = factor / total
        block = iota((n, lanes), 1) >> (pairs.bit_length() - 1)
        weights = []
        for g in range(n // per):
            pick = block + g * per == iota((n, lanes), 0)
            row = jnp.sum(jnp.where(pick, factor, 0.0), axis=0, keepdims=True)
            weights.append(jnp.where(eye, row, 0.0))
        weights = jnp.concatenate(weights, axis=1)
        high = weights.astype(BF16)
        low = (weights - high.astype(F32)).astype(BF16)
        both = dot(jnp.concatenate([high, low], axis=0), sums_ref[...])
        values = both[:pairs] + both[pairs:]
        return values, peak, total

    heard = len(apeers) + len(beside) + middle.astype(jnp.int32) * len(bpeers)
    heard += centre.astype(jnp.int32) + border.astype(jnp.int32) * len(opposite)
    pl.semaphore_wait(barrier, heard)
    pl.when(middle)(functools.partial(tell, parity_sem, [grid(z - 2 + 4 * upper)]))
    pl.when(centre)(functools.partial(tell, other_sem, [grid((nz - 1) * upper)]))

    put(asum, astat, values, as_row(peak), as_row(total))
    acopies = exchange(asum, astat, apeers, asend, arecv)
    l_wo.wait()
    turned[...] = wo[...].T
    for copy in acopies:
        copy.wait_recv()
    values, peak, total = combine(asum, astat, 2 * ny, False)
    put(bsum, bstat, values, peak, total)
    pl.when(jnp.logical_not(middle))(lambda: pl.semaphore_wait(parity_sem, 1))
    bcopies = exchange(bsum, bstat, bpeers, bsend, brecv)
    pl.when(end)(lambda: pl.semaphore_wait(other_sem, 1))

    @pl.when(border)
    def _():
        tell(border_sem, opposite)
        pl.semaphore_wait(border_sem, len(opposite))
        tell(run_sem, run)

    for copy in bcopies:
        copy.wait_recv()
    values, peak, total = combine(bsum, bstat, nz // 2, True)
    mixed[...] = values
    wide = [mixed[pl.ds(h, rows, stride=heads), :] for h in range(heads)]
    term = dot(jnp.concatenate(wide, axis=1).astype(BF16), turned[...])
    terms[pl.ds(0, rows), :] = term[:, :lanes]
    terms[pl.ds(rows, rows), :] = jnp.concatenate(
        [term[:, lanes:], jnp.zeros((rows, 2 * lanes - term.shape[1]), F32)], axis=1
    )

    def send_terms(first, peers):
        for k, peer in enumerate(peers):
            pltpu.make_async_remote_copy(
                src_ref=terms.at[pl.ds(0, 2 * rows)],
                dst_ref=terms.at[pl.ds((first + k) * 2 * rows, 2 * rows)],
                send_sem=hsend.at[0], recv_sem=hrecv.at[0], device_id=peer, device_id_type=MESH,
            ).start()

    pl.when(half == 0)(functools.partial(send_terms, 1 + len(distant), beside))
    pl.when(jnp.logical_not(border))(lambda: pl.semaphore_wait(run_sem, 1))
    for x in range(nhead // 4):
        for c in (1, 0):
            k, j = lax.rem(x - column + nhead // 4, nhead // 4), lax.rem(c - core + 2, 2)
            pltpu.make_async_remote_copy(
                src_ref=terms.at[pl.ds(0, 2 * rows)],
                dst_ref=terms.at[pl.ds(pl.multiple_of((1 + 2 * k + j) * 2 * rows, 2 * rows), 2 * rows)],
                send_sem=hsend.at[0], recv_sem=hrecv.at[0],
                device_id={"ctx": ctx, "head": x * 4 + (1 - half) * 2 + c}, device_id_type=MESH,
            ).start()
    pl.when(half == 1)(functools.partial(send_terms, 1 + len(distant), beside))
    others = terms.at[pl.ds(2 * rows, (nhead - 1) * 2 * rows)]
    hcopy = pltpu.make_async_remote_copy(
        src_ref=others, dst_ref=others, send_sem=hsend.at[0], recv_sem=hrecv.at[0],
        device_id=beside[0], device_id_type=MESH,
    )
    hcopy.wait_recv()
    whole = sum(terms[pl.ds(k * 2 * rows, 2 * rows), :] for k in range(nhead))
    whole = jnp.concatenate([whole[:rows], whole[rows:]], axis=1)
    out_ref[...] = whole[:, : out_ref.shape[1]].astype(out_ref.dtype)
    for copy in acopies + bcopies + [hcopy]:
        copy.wait_send()


def on_device(ny, nz, nhead, q_nope, q_rope, latent_cache, rope_keys, lengths, w_uk, w_uv, w_o):
    rows, heads = q_nope.shape[0], w_uk.shape[0]
    pairs, vwidth, width = rows * heads, w_uv.shape[2], w_o.shape[1]
    w_o = w_o.T
    args = (q_nope, q_rope, latent_cache, rope_keys, lengths, w_uk, w_uv, w_o)
    scratch = [
        pltpu.SMEM(a.shape, a.dtype) if a is lengths else pltpu.VMEM(a.shape, a.dtype) for a in args
    ]
    scratch += [
        pltpu.VMEM((w_uv.shape[1] // 128, pairs, 128), F32),
        pltpu.VMEM((pairs, vwidth), F32),
        pltpu.VMEM(w_o.shape[::-1], BF16),
        pltpu.VMEM((2 * ny * pairs, vwidth), BF16),
        pltpu.VMEM((2 * ny, 256), F32),
        pltpu.VMEM((nz // 2 * pairs, vwidth), BF16),
        pltpu.VMEM((nz // 2, 256), F32),
        pltpu.VMEM((nhead * 2 * rows, 128), F32),
        *[pltpu.SemaphoreType.REGULAR] * 4,
        pltpu.SemaphoreType.DMA((len(args) + rows // 2 + heads // 4 - 2,)),
    ]
    for n in (2, 2, 1):
        scratch += [pltpu.SemaphoreType.DMA((n,))] * 2
    return pl.pallas_call(
        functools.partial(kernel, ny, nz, nhead),
        out_shape=jax.ShapeDtypeStruct((rows, width), BF16),
        in_specs=[pl.BlockSpec(memory_space=pl.ANY)] * len(args),
        out_specs=pl.BlockSpec(memory_space=pltpu.VMEM),
        scratch_shapes=scratch,
        compiler_params=pltpu.CompilerParams(
            collective_id=0, has_side_effects=True, vmem_limit_bytes=32 * 1024 * 1024
        ),
        name="decode",
    )(*(pltpu.with_memory_space_constraint(a, pltpu.HBM) for a in args))


def solution(mesh):
    placed = (
        P(None, "head"),
        P(None, "head"),
        P(None, "ctx", None),
        P(None, None, "ctx"),
        P(),
        P("head", None, None),
        P("head", None, None),
        P("head", "ctx"),
    )
    nhead, nctx = mesh.shape["head"], mesh.shape["ctx"]
    ny = 4
    body = functools.partial(on_device, ny, nctx // ny, nhead)
    return jax.shard_map(
        body, mesh=mesh, in_specs=placed, out_specs=P(None, "ctx"), check_vma=False
    )
```
